256 devices in a mesh: samp: 32 (over z_hi, y, core), tp: 8 (over z_lo, x).
Axes of the slice: x: 4, y: 4, z: 8 (z_hi: 4, z_lo: 2; z = z_hi * 2 + z_lo), core: 2. Of those that a mesh axis runs over, the one named last changes fastest.
Arguments:
- queries: bfloat16 [12288, 32, 128], P('samp', 'tp'), may hold values from -9 to 9
- cache: bfloat16 [32, 1024, 8, 256], P('samp', None, 'tp'), may hold values from -6 to 6
- new_kv: bfloat16 [12288, 8, 256], P('samp', 'tp'), may hold values from -6 to 6
- slot_prompt: int32 [32], replicated, may hold values from 0 to 31, each once
- residual: bfloat16 [12288, 8192], P(('samp', 'tp')), may hold values from -60 to 60
- out_weight: bfloat16 [4096, 8192], P('tp'), may hold values from -0.5 to 0.5
- gain: float32 [8192], replicated, may hold values from 0.1 to 1.9
Outputs:
- hidden: bfloat16 [12288, 8192], P(('samp', 'tp'))
- normed: bfloat16 [12288, 8192], P(('samp', 'tp'))
The draws below stay inside these ranges and needn't reach their ends.
Inputs may be any that keep to these rules, and one draw needn't show every extreme that they name: `slot_prompt`: every prompt stands in exactly one slot.
All inputs are finite; a program needn't handle non-finite values.
Results may differ from the reference program's by a relative error of at most 0.017.
Values may be sent and summed in bfloat16 or wider, within the bound.
A program may use at most 128 MiB of HBM per device.

```python
import jax
import jax.numpy as jnp
from jax import lax

D = 8192
QH = 32
KVH = 8
HD = 128
LEN = 1024
SPD = 4
STEPS = 3
PROMPTS = 32
ROWS = 12288
N_SAMP = 32


def draw_queries(key, part):
    key = jax.random.fold_in(key, 11)
    shape = (ROWS, QH, HD)
    values = 2.0 * jax.random.normal(key, shape, jnp.float32)
    return jnp.clip(values, -9.0, 9.0).astype(jnp.bfloat16)


def draw_cache(key, part):
    key = jax.random.fold_in(key, 12)
    shape = (PROMPTS, LEN, KVH, 2 * HD)
    values = jax.random.normal(key, shape, jnp.float32)
    return jnp.clip(values, -6.0, 6.0).astype(jnp.bfloat16)


def draw_residual(key, part):
    key = jax.random.fold_in(key, 13)
    row_key, column_key, value_key = jax.random.split(key, 3)
    low = jnp.log(0.3)
    high = jnp.log(3.0)
    row_scale = jnp.exp(jax.random.uniform(row_key, (ROWS, 1), jnp.float32, low, high))
    column_scale = jnp.exp(jax.random.uniform(column_key, (1, D), jnp.float32, low, high))
    values = jnp.clip(jax.random.normal(value_key, (ROWS, D), jnp.float32), -5.0, 5.0)
    return (values * row_scale * column_scale).astype(jnp.bfloat16)


def block_levels(rng, extent, shards, low, largest):
    def one(axis_at, blocks):
        draws = jax.random.uniform(jax.random.fold_in(jax.random.fold_in(rng, 6), axis_at), (blocks,), jnp.float32, low / len(shards), largest / len(shards))
        return jnp.repeat(jnp.exp(draws), extent[axis_at] // blocks).reshape((-1,) + (1,) * (len(extent) - axis_at - 1))

    level = one(*shards[0])
    for cut in shards[1:]:
        level = level * one(*cut)
    return level


def scatter_about(rng, dims, scale, reach, pieces=(), held_as=jnp.bfloat16):
    result = jax.random.normal(rng, dims, jnp.float32) * scale
    if len(pieces) > 0:
        result = block_levels(rng, dims, pieces, -0.22, 0.18) * result
    return jnp.clip(result, min=-reach, max=reach).astype(held_as)


def setup_inputs(seed: int = 0) -> dict:
    key_list = jax.random.split(jax.random.key(seed), 8)
    queries = draw_queries(jax.random.fold_in(key_list[7], 71), 0)
    cache = draw_cache(jax.random.fold_in(key_list[7], 71), 0)
    new_kv = scatter_about(key_list[2], (ROWS, KVH, 2 * HD), 1.0, 6.0, ((0, 32), (1, 8)))
    slot_prompt = jax.random.permutation(key_list[3], PROMPTS).astype(jnp.int32)
    residual = draw_residual(jax.random.fold_in(key_list[7], 71), 0)
    out_weight = scatter_about(key_list[5], (QH * HD, D), 0.08, 0.5, ((0, 8),))
    gain = jnp.clip(1.0 + 0.18 * jax.random.normal(key_list[6], (D,), jnp.float32), 0.1, 1.9)
    return dict(queries=queries, cache=cache, new_kv=new_kv, slot_prompt=slot_prompt, residual=residual, out_weight=out_weight, gain=gain)


def attend_prompt(inputs):
    query_grid, prompt_kv, own_kv = inputs
    score_scale = 1.0 / jnp.sqrt(jnp.float32(HD))
    query_f = query_grid.astype(jnp.float32)
    prompt_keys = prompt_kv[..., :HD].astype(jnp.float32)
    prompt_values = prompt_kv[..., HD:].astype(jnp.float32)
    own_keys = own_kv[..., :HD].astype(jnp.float32)
    own_values = own_kv[..., HD:].astype(jnp.float32)
    score_prompt = jnp.einsum('nsthgd,lhd->nsthgl', query_f, prompt_keys) * score_scale
    score_own = jnp.einsum('nsthgd,nsuhd->nsthgu', query_f, own_keys) * score_scale
    step_index = jnp.arange(STEPS)
    causal_mask = (step_index[None, :] <= step_index[:, None])[None, None, :, None, None, :]
    score_own = jnp.where(causal_mask, score_own, -jnp.inf)
    maximum = jnp.maximum(lax.optimization_barrier(jnp.max(score_prompt, -1)), lax.optimization_barrier(jnp.max(score_own, -1)))
    weight_prompt = jnp.exp(score_prompt - maximum[..., None])
    weight_own = jnp.exp(score_own - maximum[..., None])
    denominator = lax.optimization_barrier(jnp.sum(weight_prompt, -1)) + lax.optimization_barrier(jnp.sum(weight_own, -1))
    weight_prompt = weight_prompt.astype(jnp.bfloat16).astype(jnp.float32)
    weight_own = weight_own.astype(jnp.bfloat16).astype(jnp.float32)
    summed = jnp.einsum('nsthgl,lhd->nsthgd', weight_prompt, prompt_values)
    summed = summed + jnp.einsum('nsthgu,nsuhd->nsthgd', weight_own, own_values)
    return (summed / denominator[..., None]).astype(jnp.bfloat16)

def reference(queries, cache, new_kv, slot_prompt, residual, out_weight, gain):
    group_size = QH // KVH
    by_prompt = jnp.zeros_like(cache).at[slot_prompt].set(cache)
    query_grid = queries.reshape(N_SAMP, PROMPTS, SPD, STEPS, KVH, group_size, HD)
    own_grid = new_kv.reshape(N_SAMP, PROMPTS, SPD, STEPS, KVH, 2 * HD)
    query_grid = jnp.moveaxis(query_grid, 1, 0)
    own_grid = jnp.moveaxis(own_grid, 1, 0)
    attended = lax.map(attend_prompt, (query_grid, by_prompt, own_grid))
    attended = jnp.moveaxis(attended, 0, 1).reshape(ROWS, QH * HD)
    projected = jnp.dot(attended, out_weight, preferred_element_type=jnp.float32)
    hidden = (residual.astype(jnp.float32) + projected).astype(jnp.bfloat16)
    hidden_f = hidden.astype(jnp.float32)
    spread = jnp.sqrt(lax.optimization_barrier(jnp.mean(hidden_f * hidden_f, -1)) + 1e-05)
    normed = (hidden_f / spread[:, None] * gain[None, :]).astype(jnp.bfloat16)
    return (hidden, normed)
```

```python
import math

import jax
import jax.numpy as jnp
from jax import lax
from jax.experimental import pallas as pl
from jax.experimental.pallas import tpu as pltpu
from jax.sharding import PartitionSpec as P

STEPS = 3
SOURCES_PER_BLOCK = 8


def attend_kernel(group_size, sent_ref, cache_ref, out_ref):
    sources, width, head_size = sent_ref.shape
    query_rows = out_ref.shape[1]
    own_rows = width - query_rows
    factor = math.log2(math.e) / math.sqrt(head_size)
    nt = (((1,), (1,)), ((), ()))
    nn = (((1,), (0,)), ((), ()))
    query = sent_ref[:, :query_rows, :].reshape(sources * query_rows, head_size)
    own = sent_ref[:, query_rows:, :].astype(jnp.float32)
    own = own.reshape(sources * own_rows, head_size).astype(jnp.bfloat16)
    total_own = sources * own_rows
    at = lax.broadcasted_iota(jnp.int32, (total_own, total_own), 0)
    taken = lax.broadcasted_iota(jnp.int32, (total_own, total_own), 1)
    move = jnp.where((taken == at + 1) & (lax.rem(at, 2) == 0), 1.0, 0.0).astype(jnp.bfloat16)
    own_value = lax.dot_general(move, own, nn, preferred_element_type=jnp.float32)
    own_value = own_value.astype(jnp.bfloat16)
    prompt_score = lax.dot_general(
        query, cache_ref[:, :head_size], nt, preferred_element_type=jnp.float32
    )
    own_score = lax.dot_general(query, own, nt, preferred_element_type=jnp.float32)
    row = lax.broadcasted_iota(jnp.int32, own_score.shape, 0) // group_size
    column = lax.broadcasted_iota(jnp.int32, own_score.shape, 1)
    key = column // 2
    seen = (lax.rem(column, 2) == 0) & (key <= row) & (key >= row - lax.rem(row, STEPS))
    own_score = jnp.where(seen, own_score, -jnp.inf)
    maximum = jnp.maximum(
        jnp.max(prompt_score, -1, keepdims=True), jnp.max(own_score, -1, keepdims=True)
    )
    shift = maximum * factor
    prompt_weight = jnp.exp2(prompt_score * factor - shift)
    own_weight = jnp.exp2(own_score * factor - shift)
    denominator = jnp.sum(prompt_weight, -1, keepdims=True) + jnp.sum(
        own_weight, -1, keepdims=True
    )
    summed = lax.dot_general(
        prompt_weight.astype(jnp.bfloat16),
        cache_ref[:, head_size:],
        nn,
        preferred_element_type=jnp.float32,
    )
    summed = summed + lax.dot_general(
        own_weight.astype(jnp.bfloat16), own_value, nn, preferred_element_type=jnp.float32
    )
    attended = (summed / denominator).astype(jnp.bfloat16)
    out_ref[...] = attended.reshape(sources, query_rows, head_size)


def attend(sent, cache, query_rows, group_size):
    sources, width, head_size = sent.shape
    block = min(SOURCES_PER_BLOCK, sources)
    return pl.pallas_call(
        lambda *refs: attend_kernel(group_size, *refs),
        grid=(sources // block,),
        in_specs=[
            pl.BlockSpec((block, width, head_size), lambda i: (i, 0, 0)),
            pl.BlockSpec(cache.shape, lambda i: (0, 0)),
        ],
        out_specs=pl.BlockSpec((block, query_rows, head_size), lambda i: (i, 0, 0)),
        out_shape=jax.ShapeDtypeStruct((sources, query_rows, head_size), jnp.bfloat16),
        compiler_params=pltpu.CompilerParams(vmem_limit_bytes=40 * 2**20),
    )(sent, cache)


def on_device(queries, cache, new_kv, slot_prompt, residual, out_weight, gain):
    row_total, heads_local, head_size = queries.shape
    group_size = heads_local // new_kv.shape[1]
    prompt_count = slot_prompt.shape[0]
    rows = row_total // prompt_count
    packed = jnp.concatenate(
        [
            queries.reshape(prompt_count, rows * heads_local, head_size),
            new_kv.reshape(prompt_count, rows * 2, head_size),
        ],
        axis=1,
    )
    sent = jnp.take(packed, slot_prompt, axis=0)
    sent = lax.all_to_all(sent, "samp", 0, 0, tiled=True)
    attended = attend(sent, cache.reshape(cache.shape[1], 2 * head_size), rows * heads_local, group_size)
    attended = lax.all_to_all(attended, "samp", 0, 0, tiled=True)
    slot_of = jnp.zeros_like(slot_prompt).at[slot_prompt].set(jnp.arange(prompt_count, dtype=jnp.int32))
    attended = jnp.take(attended, slot_of, axis=0).reshape(row_total, heads_local * head_size)
    projected = lax.psum_scatter(
        jnp.dot(attended, out_weight, preferred_element_type=jnp.float32).astype(jnp.bfloat16),
        "tp",
        scatter_dimension=0,
        tiled=True,
    ).astype(jnp.float32)
    hidden = (residual.astype(jnp.float32) + projected).astype(jnp.bfloat16)
    hidden_f = hidden.astype(jnp.float32)
    spread = jnp.sqrt(jnp.mean(hidden_f * hidden_f, -1) + 1e-05)
    normed = (hidden_f / spread[:, None] * gain[None, :]).astype(jnp.bfloat16)
    return (hidden, normed)


def solution(mesh):
    placed = (
        P("samp", "tp", None),
        P("samp", None, "tp", None),
        P("samp", "tp", None),
        P(),
        P(("samp", "tp"), None),
        P("tp", None),
        P(),
    )
    return jax.shard_map(
        on_device,
        mesh=mesh,
        in_specs=placed,
        out_specs=(P(("samp", "tp"), None), P(("samp", "tp"), None)),
        check_vma=False,
    )
```

```python
import math

import jax
import jax.numpy as jnp
from jax import lax
from jax.experimental import pallas as pl
from jax.experimental.pallas import tpu as pltpu
from jax.sharding import PartitionSpec as P

STEPS = 3
SOURCES_PER_BLOCK = 8


def attend_kernel(group_size, sent_ref, cache_ref, out_ref):
    sources, width, head_size = sent_ref.shape
    query_rows = out_ref.shape[1]
    own_rows = width - query_rows
    factor = math.log2(math.e) / math.sqrt(head_size)
    nt = (((1,), (1,)), ((), ()))
    nn = (((1,), (0,)), ((), ()))
    query = sent_ref[:, :query_rows, :].reshape(sources * query_rows, head_size)
    own = sent_ref[:, query_rows:, :].astype(jnp.float32)
    own = own.reshape(sources * own_rows, head_size).astype(jnp.bfloat16)
    total_own = sources * own_rows
    at = lax.broadcasted_iota(jnp.int32, (total_own, total_own), 0)
    taken = lax.broadcasted_iota(jnp.int32, (total_own, total_own), 1)
    move = jnp.where((taken == at + 1) & (lax.rem(at, 2) == 0), 1.0, 0.0).astype(jnp.bfloat16)
    own_value = lax.dot_general(move, own, nn, preferred_element_type=jnp.float32)
    own_value = own_value.astype(jnp.bfloat16)
    prompt_score = lax.dot_general(
        query, cache_ref[:, :head_size], nt, preferred_element_type=jnp.float32
    )
    own_score = lax.dot_general(query, own, nt, preferred_element_type=jnp.float32)
    row = lax.broadcasted_iota(jnp.int32, own_score.shape, 0) // group_size
    column = lax.broadcasted_iota(jnp.int32, own_score.shape, 1)
    key = column // 2
    seen = (lax.rem(column, 2) == 0) & (key <= row) & (key >= row - lax.rem(row, STEPS))
    own_score = jnp.where(seen, own_score, -jnp.inf)
    maximum = jnp.maximum(
        jnp.max(prompt_score, -1, keepdims=True), jnp.max(own_score, -1, keepdims=True)
    )
    shift = maximum * factor
    prompt_weight = jnp.exp2(prompt_score * factor - shift)
    own_weight = jnp.exp2(own_score * factor - shift)
    denominator = jnp.sum(prompt_weight, -1, keepdims=True) + jnp.sum(
        own_weight, -1, keepdims=True
    )
    summed = lax.dot_general(
        prompt_weight.astype(jnp.bfloat16),
        cache_ref[:, head_size:],
        nn,
        preferred_element_type=jnp.float32,
    )
    summed = summed + lax.dot_general(
        own_weight.astype(jnp.bfloat16), own_value, nn, preferred_element_type=jnp.float32
    )
    attended = (summed / denominator).astype(jnp.bfloat16)
    out_ref[...] = attended.reshape(sources, query_rows, head_size)


def attend(sent, cache, query_rows, group_size):
    sources, width, head_size = sent.shape
    block = min(SOURCES_PER_BLOCK, sources)
    return pl.pallas_call(
        lambda *refs: attend_kernel(group_size, *refs),
        grid=(sources // block,),
        in_specs=[
            pl.BlockSpec((block, width, head_size), lambda i: (i, 0, 0)),
            pl.BlockSpec(cache.shape, lambda i: (0, 0)),
        ],
        out_specs=pl.BlockSpec((block, query_rows, head_size), lambda i: (i, 0, 0)),
        out_shape=jax.ShapeDtypeStruct((sources, query_rows, head_size), jnp.bfloat16),
        compiler_params=pltpu.CompilerParams(vmem_limit_bytes=40 * 2**20),
    )(sent, cache)


RING = 4
RING_FIRST = 5
PAIR_FIRST = 3


def project_kernel(
    attended_ref,
    weight_hbm,
    out_ref,
    weight,
    weight_sem,
    xp,
    xr,
    xq,
    zp,
    zq,
    zr,
    xr_send,
    xr_recv,
    xq_send,
    xq_recv,
    zq_send,
    zq_recv,
    zr_send,
    zr_recv,
):
    rows = out_ref.shape[0]
    width = weight.shape[2]
    chunks = weight.shape[0]
    here = lax.axis_index("tp")
    x = lax.rem(here, RING)
    z = here // RING
    other = 1 - z

    def ring_device(way):
        step = 1 if way == 0 else RING - 1
        return {"tp": z * RING + lax.rem(x + step, RING)}

    pair_device = {"tp": other * RING + x}

    def block(way, step):
        ahead = 2 * RING - 1 - step if way == 0 else 1 + step
        return lax.rem(x + ahead, RING)

    def ring_chunk(k, way):
        return 2 * k + way

    def pair_chunk(k, way):
        return 2 * RING_FIRST + 2 * k + way

    def fetch(chunk):
        return pltpu.make_async_copy(
            weight_hbm.at[:, pl.ds(chunk * width, width)], weight.at[chunk], weight_sem.at[chunk]
        )

    def remote(src, dst, send, recv, device):
        return pltpu.make_async_remote_copy(
            src_ref=src,
            dst_ref=dst,
            send_sem=send,
            recv_sem=recv,
            device_id=device,
            device_id_type=pl.DeviceIdType.MESH,
        )

    def ring_copy(k, way, step):
        return remote(
            xp.at[way, k, block(way, step)],
            xr.at[way, k, step],
            xr_send.at[way, k, step],
            xr_recv.at[way, k, step],
            ring_device(way),
        )

    def ring_pair_copy(k, way):
        return remote(
            xp.at[way, k, x, other],
            xq.at[way, k],
            xq_send.at[way, k],
            xq_recv.at[way, k],
            pair_device,
        )

    def pair_copy(k, way):
        return remote(
            zp.at[way, k, other],
            zq.at[way, k],
            zq_send.at[way, k],
            zq_recv.at[way, k],
            pair_device,
        )

    def pair_ring_copy(k, way, step):
        return remote(
            zp.at[way, k, z, block(way, step)],
            zr.at[way, k, step],
            zr_send.at[way, k, step],
            zr_recv.at[way, k, step],
            ring_device(way),
        )

    def multiply(chunk):
        fetch(chunk).wait()
        product = jnp.dot(
            attended_ref[...], weight[chunk], preferred_element_type=jnp.float32
        )
        return product.astype(jnp.bfloat16)

    def start_ring(k):
        for way in range(2):
            product = multiply(ring_chunk(k, way))
            for j in range(2 * RING):
                xp[way, k, j % RING, j // RING] = product[j * rows : (j + 1) * rows]
            ring_copy(k, way, 0).start()

    def start_pair(k):
        for way in range(2):
            product = multiply(pair_chunk(k, way))
            for j in range(2 * RING):
                zp[way, k, j // RING, j % RING] = product[j * rows : (j + 1) * rows]
            pair_copy(k, way).start()

    def wide(value):
        return value.astype(jnp.float32)

    def ring_step(k, step):
        for way in range(2):
            ring_copy(k, way, step).wait_recv()
            at = block(way, step + 1)
            xp[way, k, at] = (wide(xp[way, k, at]) + wide(xr[way, k, step])).astype(jnp.bfloat16)
            if step < RING - 2:
                ring_copy(k, way, step + 1).start()
            else:
                ring_pair_copy(k, way).start()

    def ring_end(k):
        for way in range(2):
            ring_pair_copy(k, way).wait_recv()
            columns = pl.ds(ring_chunk(k, way) * width, width)
            out_ref[:, columns] = (wide(xp[way, k, x, z]) + wide(xq[way, k])).astype(jnp.bfloat16)

    def pair_step(k):
        for way in range(2):
            pair_copy(k, way).wait_recv()
            at = block(way, 0)
            zp[way, k, z, at] = (wide(zp[way, k, z, at]) + wide(zq[way, k, at])).astype(
                jnp.bfloat16
            )
            pair_ring_copy(k, way, 0).start()

    def pair_ring_step(k, step):
        for way in range(2):
            pair_ring_copy(k, way, step).wait_recv()
            at = block(way, step + 1)
            total = wide(zp[way, k, z, at]) + wide(zq[way, k, at]) + wide(zr[way, k, step])
            if step < RING - 2:
                zp[way, k, z, at] = total.astype(jnp.bfloat16)
                pair_ring_copy(k, way, step + 1).start()
            else:
                columns = pl.ds(pair_chunk(k, way) * width, width)
                out_ref[:, columns] = total.astype(jnp.bfloat16)

    order = []
    for k in range(max(RING_FIRST, PAIR_FIRST)):
        order += [pair_chunk(k, way) for way in range(2)] if k < PAIR_FIRST else []
        order += [ring_chunk(k, way) for way in range(2)] if k < RING_FIRST else []
    for chunk in order:
        fetch(chunk).start()
    barrier = pltpu.get_barrier_semaphore()
    for device in (ring_device(0), ring_device(1), pair_device):
        pl.semaphore_signal(
            barrier, inc=1, device_id=device, device_id_type=pl.DeviceIdType.MESH
        )
    pl.semaphore_wait(barrier, 3)

    for k in range(max(RING_FIRST, PAIR_FIRST)):
        if k < PAIR_FIRST:
            start_pair(k)
        if k < RING_FIRST:
            start_ring(k)
    steps = []
    for k in range(RING_FIRST):
        for step in range(RING - 1):
            steps.append((step + (k + 1) / RING_FIRST, 0, k, step))
        steps.append((3.2 + (k + 1) * 1.0 / RING_FIRST, 1, k, 0))
    for k in range(PAIR_FIRST):
        arrival = 3.0 * (k + 1) / PAIR_FIRST
        steps.append((arrival, 2, k, 0))
        for step in range(RING - 1):
            steps.append((arrival + 0.45 * (step + 1), 3, k, step))
    for _, kind, k, step in sorted(steps):
        if kind == 0:
            ring_step(k, step)
        elif kind == 1:
            ring_end(k)
        elif kind == 2:
            pair_step(k)
        else:
            pair_ring_step(k, step)
    for way in range(2):
        for k in range(RING_FIRST):
            for step in range(RING - 1):
                ring_copy(k, way, step).wait_send()
            ring_pair_copy(k, way).wait_send()
        for k in range(PAIR_FIRST):
            pair_copy(k, way).wait_send()
            for step in range(RING - 1):
                pair_ring_copy(k, way, step).wait_send()


def project(attended, out_weight):
    total, depth = attended.shape
    columns = out_weight.shape[1]
    rows = total // (2 * RING)
    chunks = 2 * (RING_FIRST + PAIR_FIRST)
    width = columns // chunks
    steps = RING - 1
    dma = pltpu.SemaphoreType.DMA
    held = jnp.bfloat16
    return pl.pallas_call(
        project_kernel,
        in_specs=[
            pl.BlockSpec(memory_space=pltpu.VMEM),
            pl.BlockSpec(memory_space=pl.ANY),
        ],
        out_specs=pl.BlockSpec(memory_space=pltpu.VMEM),
        out_shape=jax.ShapeDtypeStruct((rows, columns), held),
        scratch_shapes=[
            pltpu.VMEM((chunks, depth, width), held),
            dma((chunks,)),
            pltpu.VMEM((2, RING_FIRST, RING, 2, rows, width), held),
            pltpu.VMEM((2, RING_FIRST, steps, 2, rows, width), held),
            pltpu.VMEM((2, RING_FIRST, rows, width), held),
            pltpu.VMEM((2, PAIR_FIRST, 2, RING, rows, width), held),
            pltpu.VMEM((2, PAIR_FIRST, RING, rows, width), held),
            pltpu.VMEM((2, PAIR_FIRST, steps, rows, width), held),
            dma((2, RING_FIRST, steps)),
            dma((2, RING_FIRST, steps)),
            dma((2, RING_FIRST)),
            dma((2, RING_FIRST)),
            dma((2, PAIR_FIRST)),
            dma((2, PAIR_FIRST)),
            dma((2, PAIR_FIRST, steps)),
            dma((2, PAIR_FIRST, steps)),
        ],
        compiler_params=pltpu.CompilerParams(
            collective_id=0, has_side_effects=True, vmem_limit_bytes=48 * 2**20
        ),
        cost_estimate=pl.CostEstimate(
            flops=2 * total * depth * columns,
            bytes_accessed=2 * (depth * columns + total * depth + rows * columns),
            transcendentals=0,
        ),
    )(attended, out_weight)


def on_device(queries, cache, new_kv, slot_prompt, residual, out_weight, gain):
    row_total, heads_local, head_size = queries.shape
    group_size = heads_local // new_kv.shape[1]
    prompt_count = slot_prompt.shape[0]
    rows = row_total // prompt_count
    packed = jnp.concatenate(
        [
            queries.reshape(prompt_count, rows * heads_local, head_size),
            new_kv.reshape(prompt_count, rows * 2, head_size),
        ],
        axis=1,
    )
    sent = jnp.take(packed, slot_prompt, axis=0)
    sent = lax.all_to_all(sent, "samp", 0, 0, tiled=True)
    attended = attend(sent, cache.reshape(cache.shape[1], 2 * head_size), rows * heads_local, group_size)
    attended = lax.all_to_all(attended, "samp", 0, 0, tiled=True)
    slot_of = jnp.zeros_like(slot_prompt).at[slot_prompt].set(jnp.arange(prompt_count, dtype=jnp.int32))
    attended = jnp.take(attended, slot_of, axis=0).reshape(row_total, heads_local * head_size)
    projected = project(attended, out_weight).astype(jnp.float32)
    hidden = (residual.astype(jnp.float32) + projected).astype(jnp.bfloat16)
    hidden_f = hidden.astype(jnp.float32)
    spread = jnp.sqrt(jnp.mean(hidden_f * hidden_f, -1) + 1e-05)
    normed = (hidden_f / spread[:, None] * gain[None, :]).astype(jnp.bfloat16)
    return (hidden, normed)


def solution(mesh):
    placed = (
        P("samp", "tp", None),
        P("samp", None, "tp", None),
        P("samp", "tp", None),
        P(),
        P(("samp", "tp"), None),
        P("tp", None),
        P(),
    )
    return jax.shard_map(
        on_device,
        mesh=mesh,
        in_specs=placed,
        out_specs=(P(("samp", "tp"), None), P(("samp", "tp"), None)),
        check_vma=False,
    )
```

```python
import functools
import math

import jax
import jax.numpy as jnp
from jax import lax
from jax.experimental import pallas as pl
from jax.experimental.pallas import tpu as pltpu
from jax.sharding import PartitionSpec as P

STEPS = 3
Z_HI = 4
Y = 4
CORES = 2
GROUP = Y * CORES
OWN = 16


def exchange_kernel(
    heads,
    slot_prompt_ref,
    query_ref,
    own_ref,
    cache_ref,
    out_ref,
    sent,
    held,
    done,
    back,
    slot_of,
    sent_sem,
    held_sem,
    done_sem,
    back_sem,
):
    prompts, query_rows, head_size = query_ref.shape
    width = sent.shape[1]
    here = lax.axis_index("samp")
    here_z = here // GROUP
    here_y = lax.rem(here, GROUP) // CORES
    here_core = lax.rem(here, CORES)

    def z_distance(group):
        return lax.rem(group * (group + 1) // 2, Z_HI)

    def partner(group, member, away):
        dz = z_distance(group)
        dy = member // CORES
        dcore = lax.rem(member, CORES)
        if not away:
            dz = Z_HI - dz
            dy = Y - dy
        z = lax.rem(here_z + dz, Z_HI)
        y = lax.rem(here_y + dy, Y)
        core = lax.rem(here_core + dcore, CORES)
        return z * GROUP + y * CORES + core

    def remote(src, dst, send, recv, device):
        return pltpu.make_async_remote_copy(
            src_ref=src,
            dst_ref=dst,
            send_sem=send,
            recv_sem=recv,
            device_id={"samp": device},
            device_id_type=pl.DeviceIdType.MESH,
        )

    def fill(group, member, into):
        slot = partner(group, member, True)
        prompt = slot_prompt_ref[slot]
        at = group * GROUP + member
        into[at, :query_rows] = query_ref[prompt]
        own = own_ref[prompt]
        into[at, query_rows : query_rows + OWN] = own[:, :head_size]
        into[at, query_rows + OWN :] = own[:, head_size:]

    barrier = pltpu.get_barrier_semaphore()

    def greet(at, carry):
        pl.semaphore_signal(
            barrier,
            inc=1,
            device_id={"samp": partner(at // GROUP, lax.rem(at, GROUP), True)},
            device_id_type=pl.DeviceIdType.MESH,
        )
        return carry

    lax.fori_loop(1, prompts, greet, 0)
    fill(0, 0, held)

    def prepare(at, carry):
        fill(at // GROUP, lax.rem(at, GROUP), sent)
        return carry

    lax.fori_loop(1, prompts, prepare, 0)

    def send_out(at, carry):
        group = at // GROUP
        remote(
            sent.at[at],
            held.at[at],
            sent_sem,
            held_sem.at[group],
            partner(group, lax.rem(at, GROUP), True),
        ).start()
        return carry

    pl.semaphore_wait(barrier, prompts - 1)
    for group in range(Z_HI - 1, -1, -1):
        lax.fori_loop(max(1, group * GROUP), (group + 1) * GROUP, send_out, 0)

    def find(prompt, carry):
        def look(slot, found):
            return jnp.where(slot_prompt_ref[slot] == prompt, slot, found)

        slot_of[prompt] = lax.fori_loop(0, prompts, look, 0)
        return carry

    lax.fori_loop(0, prompts, find, 0)

    factor = math.log2(math.e) / math.sqrt(head_size)
    nt = (((1,), (1,)), ((), ()))
    nn = (((1,), (0,)), ((), ()))

    def attend(group, first):
        base = group * GROUP
        count = GROUP - 1 if first else GROUP
        start = base + GROUP - count
        arrived = held.at[pl.ds(start, count)]
        pltpu.make_async_copy(arrived, arrived, held_sem.at[group]).wait()
        query = held[pl.ds(base, GROUP), :query_rows].reshape(GROUP * query_rows, head_size)
        key = held[pl.ds(base, GROUP), query_rows : query_rows + OWN]
        key = key.reshape(GROUP * OWN, head_size)
        value = held[pl.ds(base, GROUP), query_rows + OWN :].reshape(GROUP * OWN, head_size)
        prompt_score = lax.dot_general(
            query, cache_ref[:, :head_size], nt, preferred_element_type=jnp.float32
        )
        own_score = lax.dot_general(query, key, nt, preferred_element_type=jnp.float32)
        line = lax.broadcasted_iota(jnp.int32, own_score.shape, 0)
        column = lax.broadcasted_iota(jnp.int32, own_score.shape, 1)
        row = lax.rem(line, query_rows) // heads
        own = lax.rem(column, OWN)
        seen = (line // query_rows == column // OWN) & (own <= row)
        seen = seen & (own >= row - lax.rem(row, STEPS))
        own_score = jnp.where(seen, own_score, -jnp.inf)
        maximum = jnp.maximum(
            jnp.max(prompt_score, -1, keepdims=True), jnp.max(own_score, -1, keepdims=True)
        )
        shift = maximum * factor
        prompt_weight = jnp.exp2(prompt_score * factor - shift)
        own_weight = jnp.exp2(own_score * factor - shift)
        denominator = jnp.sum(prompt_weight, -1, keepdims=True) + jnp.sum(
            own_weight, -1, keepdims=True
        )
        summed = lax.dot_general(
            prompt_weight.astype(jnp.bfloat16),
            cache_ref[:, head_size:],
            nn,
            preferred_element_type=jnp.float32,
        )
        summed = summed + lax.dot_general(
            own_weight.astype(jnp.bfloat16), value, nn, preferred_element_type=jnp.float32
        )
        attended = (summed / denominator).astype(jnp.bfloat16)
        attended = attended.reshape(GROUP, query_rows, head_size)
        done[pl.ds(base, GROUP)] = attended
        if first:
            back[0] = attended[0]

        def send_back(at, carry):
            remote(
                done.at[at],
                back.at[at],
                done_sem,
                back_sem,
                partner(group, at - base, False),
            ).start()
            return carry

        lax.fori_loop(start, base + GROUP, send_back, 0)

    attend(0, True)

    def attend_next(group, carry):
        attend(group, False)
        return carry

    lax.fori_loop(1, Z_HI, attend_next, 0)
    others = sent.at[pl.ds(1, prompts - 1)]
    pltpu.make_async_copy(others, others, sent_sem).wait()
    others = done.at[pl.ds(1, prompts - 1)]
    pltpu.make_async_copy(others, others, done_sem).wait()
    others = back.at[pl.ds(1, prompts - 1)]
    pltpu.make_async_copy(others, others, back_sem).wait()

    def place(prompt, carry):
        slot = slot_of[prompt]
        dz = lax.rem(slot // GROUP - here_z + Z_HI, Z_HI)
        dy = lax.rem(lax.rem(slot, GROUP) // CORES - here_y + Y, Y)
        dcore = lax.rem(lax.rem(slot, CORES) + here_core, CORES)
        out_ref[prompt] = back[z_distance(dz) * GROUP + dy * CORES + dcore]
        return carry

    lax.fori_loop(0, prompts, place, 0)


def exchange(slot_prompt, query, own, cache, heads):
    prompts, query_rows, head_size = query.shape
    width = query_rows + 2 * OWN
    held = jnp.bfloat16
    dma = pltpu.SemaphoreType.DMA
    vmem = pl.BlockSpec(memory_space=pltpu.VMEM)
    return pl.pallas_call(
        functools.partial(exchange_kernel, heads),
        in_specs=[pl.BlockSpec(memory_space=pltpu.SMEM), vmem, vmem, vmem],
        out_specs=vmem,
        out_shape=jax.ShapeDtypeStruct(query.shape, held),
        scratch_shapes=[
            pltpu.VMEM((prompts, width, head_size), held),
            pltpu.VMEM((prompts, width, head_size), held),
            pltpu.VMEM(query.shape, held),
            pltpu.VMEM(query.shape, held),
            pltpu.SMEM((prompts,), jnp.int32),
            dma,
            dma((Z_HI,)),
            dma,
            dma,
        ],
        compiler_params=pltpu.CompilerParams(
            collective_id=1, has_side_effects=True, vmem_limit_bytes=40 * 2**20
        ),
    )(slot_prompt, query, own, cache)


RING = 4
RING_FIRST = 5
PAIR_FIRST = 3


def project_kernel(
    attended_ref,
    weight_hbm,
    out_ref,
    weight,
    weight_sem,
    xp,
    xr,
    xq,
    zp,
    zq,
    zr,
    xr_send,
    xr_recv,
    xq_send,
    xq_recv,
    zq_send,
    zq_recv,
    zr_send,
    zr_recv,
):
    rows = out_ref.shape[0]
    width = weight.shape[2]
    chunks = weight.shape[0]
    here = lax.axis_index("tp")
    x = lax.rem(here, RING)
    z = here // RING
    other = 1 - z

    def ring_device(way):
        step = 1 if way == 0 else RING - 1
        return {"tp": z * RING + lax.rem(x + step, RING)}

    pair_device = {"tp": other * RING + x}

    def block(way, step):
        ahead = 2 * RING - 1 - step if way == 0 else 1 + step
        return lax.rem(x + ahead, RING)

    def ring_chunk(k, way):
        return 2 * k + way

    def pair_chunk(k, way):
        return 2 * RING_FIRST + 2 * k + way

    def fetch(chunk):
        return pltpu.make_async_copy(
            weight_hbm.at[:, pl.ds(chunk * width, width)], weight.at[chunk], weight_sem.at[chunk]
        )

    def remote(src, dst, send, recv, device):
        return pltpu.make_async_remote_copy(
            src_ref=src,
            dst_ref=dst,
            send_sem=send,
            recv_sem=recv,
            device_id=device,
            device_id_type=pl.DeviceIdType.MESH,
        )

    def ring_copy(k, way, step):
        return remote(
            xp.at[way, k, block(way, step)],
            xr.at[way, k, step],
            xr_send.at[way, k, step],
            xr_recv.at[way, k, step],
            ring_device(way),
        )

    def ring_pair_copy(k, way):
        return remote(
            xp.at[way, k, x, other],
            xq.at[way, k],
            xq_send.at[way, k],
            xq_recv.at[way, k],
            pair_device,
        )

    def pair_copy(k, way):
        return remote(
            zp.at[way, k, other],
            zq.at[way, k],
            zq_send.at[way, k],
            zq_recv.at[way, k],
            pair_device,
        )

    def pair_ring_copy(k, way, step):
        return remote(
            zp.at[way, k, z, block(way, step)],
            zr.at[way, k, step],
            zr_send.at[way, k, step],
            zr_recv.at[way, k, step],
            ring_device(way),
        )

    def multiply(chunk):
        fetch(chunk).wait()
        product = jnp.dot(
            attended_ref[...], weight[chunk], preferred_element_type=jnp.float32
        )
        return product.astype(jnp.bfloat16)

    def start_ring(k):
        for way in range(2):
            product = multiply(ring_chunk(k, way))
            for j in range(2 * RING):
                xp[way, k, j % RING, j // RING] = product[j * rows : (j + 1) * rows]
            ring_copy(k, way, 0).start()

    def start_pair(k):
        for way in range(2):
            product = multiply(pair_chunk(k, way))
            for j in range(2 * RING):
                zp[way, k, j // RING, j % RING] = product[j * rows : (j + 1) * rows]
            pair_copy(k, way).start()

    def wide(value):
        return value.astype(jnp.float32)

    def ring_step(k, step):
        for way in range(2):
            ring_copy(k, way, step).wait_recv()
            at = block(way, step + 1)
            xp[way, k, at] = (wide(xp[way, k, at]) + wide(xr[way, k, step])).astype(jnp.bfloat16)
            if step < RING - 2:
                ring_copy(k, way, step + 1).start()
            else:
                ring_pair_copy(k, way).start()

    def ring_end(k):
        for way in range(2):
            ring_pair_copy(k, way).wait_recv()
            columns = pl.ds(ring_chunk(k, way) * width, width)
            out_ref[:, columns] = (wide(xp[way, k, x, z]) + wide(xq[way, k])).astype(jnp.bfloat16)

    def pair_step(k):
        for way in range(2):
            pair_copy(k, way).wait_recv()
            at = block(way, 0)
            zp[way, k, z, at] = (wide(zp[way, k, z, at]) + wide(zq[way, k, at])).astype(
                jnp.bfloat16
            )
            pair_ring_copy(k, way, 0).start()

    def pair_ring_step(k, step):
        for way in range(2):
            pair_ring_copy(k, way, step).wait_recv()
            at = block(way, step + 1)
            total = wide(zp[way, k, z, at]) + wide(zq[way, k, at]) + wide(zr[way, k, step])
            if step < RING - 2:
                zp[way, k, z, at] = total.astype(jnp.bfloat16)
                pair_ring_copy(k, way, step + 1).start()
            else:
                columns = pl.ds(pair_chunk(k, way) * width, width)
                out_ref[:, columns] = total.astype(jnp.bfloat16)

    order = []
    for k in range(max(RING_FIRST, PAIR_FIRST)):
        order += [pair_chunk(k, way) for way in range(2)] if k < PAIR_FIRST else []
        order += [ring_chunk(k, way) for way in range(2)] if k < RING_FIRST else []
    for chunk in order:
        fetch(chunk).start()
    barrier = pltpu.get_barrier_semaphore()
    for device in (ring_device(0), ring_device(1), pair_device):
        pl.semaphore_signal(
            barrier, inc=1, device_id=device, device_id_type=pl.DeviceIdType.MESH
        )
    pl.semaphore_wait(barrier, 3)

    for k in range(max(RING_FIRST, PAIR_FIRST)):
        if k < PAIR_FIRST:
            start_pair(k)
        if k < RING_FIRST:
            start_ring(k)
    steps = []
    for k in range(RING_FIRST):
        for step in range(RING - 1):
            steps.append((step + (k + 1) / RING_FIRST, 0, k, step))
        steps.append((3.2 + (k + 1) * 1.0 / RING_FIRST, 1, k, 0))
    for k in range(PAIR_FIRST):
        arrival = 3.0 * (k + 1) / PAIR_FIRST
        steps.append((arrival, 2, k, 0))
        for step in range(RING - 1):
            steps.append((arrival + 0.45 * (step + 1), 3, k, step))
    for _, kind, k, step in sorted(steps):
        if kind == 0:
            ring_step(k, step)
        elif kind == 1:
            ring_end(k)
        elif kind == 2:
            pair_step(k)
        else:
            pair_ring_step(k, step)
    for way in range(2):
        for k in range(RING_FIRST):
            for step in range(RING - 1):
                ring_copy(k, way, step).wait_send()
            ring_pair_copy(k, way).wait_send()
        for k in range(PAIR_FIRST):
            pair_copy(k, way).wait_send()
            for step in range(RING - 1):
                pair_ring_copy(k, way, step).wait_send()


def project(attended, out_weight):
    total, depth = attended.shape
    columns = out_weight.shape[1]
    rows = total // (2 * RING)
    chunks = 2 * (RING_FIRST + PAIR_FIRST)
    width = columns // chunks
    steps = RING - 1
    dma = pltpu.SemaphoreType.DMA
    held = jnp.bfloat16
    return pl.pallas_call(
        project_kernel,
        in_specs=[
            pl.BlockSpec(memory_space=pltpu.VMEM),
            pl.BlockSpec(memory_space=pl.ANY),
        ],
        out_specs=pl.BlockSpec(memory_space=pltpu.VMEM),
        out_shape=jax.ShapeDtypeStruct((rows, columns), held),
        scratch_shapes=[
            pltpu.VMEM((chunks, depth, width), held),
            dma((chunks,)),
            pltpu.VMEM((2, RING_FIRST, RING, 2, rows, width), held),
            pltpu.VMEM((2, RING_FIRST, steps, 2, rows, width), held),
            pltpu.VMEM((2, RING_FIRST, rows, width), held),
            pltpu.VMEM((2, PAIR_FIRST, 2, RING, rows, width), held),
            pltpu.VMEM((2, PAIR_FIRST, RING, rows, width), held),
            pltpu.VMEM((2, PAIR_FIRST, steps, rows, width), held),
            dma((2, RING_FIRST, steps)),
            dma((2, RING_FIRST, steps)),
            dma((2, RING_FIRST)),
            dma((2, RING_FIRST)),
            dma((2, PAIR_FIRST)),
            dma((2, PAIR_FIRST)),
            dma((2, PAIR_FIRST, steps)),
            dma((2, PAIR_FIRST, steps)),
        ],
        compiler_params=pltpu.CompilerParams(
            collective_id=0, has_side_effects=True, vmem_limit_bytes=48 * 2**20
        ),
        cost_estimate=pl.CostEstimate(
            flops=2 * total * depth * columns,
            bytes_accessed=2 * (depth * columns + total * depth + rows * columns),
            transcendentals=0,
        ),
    )(attended, out_weight)


def on_device(queries, cache, new_kv, slot_prompt, residual, out_weight, gain):
    row_total, heads_local, head_size = queries.shape
    prompts = slot_prompt.shape[0]
    rows = row_total // prompts
    own = jnp.pad(new_kv.reshape(prompts, rows, 2 * head_size), ((0, 0), (0, OWN - rows), (0, 0)))
    attended = exchange(
        slot_prompt,
        queries.reshape(prompts, rows * heads_local, head_size),
        own,
        cache.reshape(cache.shape[1], 2 * head_size),
        heads_local,
    )
    attended = attended.reshape(row_total, heads_local * head_size)
    projected = project(attended, out_weight).astype(jnp.float32)
    hidden = (residual.astype(jnp.float32) + projected).astype(jnp.bfloat16)
    hidden_f = hidden.astype(jnp.float32)
    spread = jnp.sqrt(jnp.mean(hidden_f * hidden_f, -1) + 1e-05)
    normed = (hidden_f / spread[:, None] * gain[None, :]).astype(jnp.bfloat16)
    return (hidden, normed)


def solution(mesh):
    placed = (
        P("samp", "tp", None),
        P("samp", None, "tp", None),
        P("samp", "tp", None),
        P(),
        P(("samp", "tp"), None),
        P("tp", None),
        P(),
    )
    return jax.shard_map(
        on_device,
        mesh=mesh,
        in_specs=placed,
        out_specs=(P(("samp", "tp"), None), P(("samp", "tp"), None)),
        check_vma=False,
    )
```

```python
import functools
import math

import jax
import jax.numpy as jnp
from jax import lax
from jax.experimental import pallas as pl
from jax.experimental.pallas import tpu as pltpu
from jax.sharding import PartitionSpec as P

STEPS = 3
Z_HI = 4
Y = 4
CORES = 2
GROUP = Y * CORES
OWN = 16


def exchange_kernel(
    heads,
    slot_prompt_ref,
    query_hbm,
    own_hbm,
    cache_hbm,
    out_ref,
    query_ref,
    own_ref,
    own_rows,
    cache_ref,
    sent,
    held,
    done,
    back,
    slot_of,
    load_sem,
    sent_sem,
    held_sem,
    done_sem,
    back_sem,
):
    prompts, query_rows, head_size = query_ref.shape
    width = sent.shape[1]
    here = lax.axis_index("samp")
    here_z = here // GROUP
    here_y = lax.rem(here, GROUP) // CORES
    here_core = lax.rem(here, CORES)

    def z_distance(group):
        return lax.rem(group * (group + 1) // 2, Z_HI)

    def partner(group, member, away):
        dz = z_distance(group)
        dy = member // CORES
        dcore = lax.rem(member, CORES)
        if not away:
            dz = Z_HI - dz
            dy = Y - dy
        z = lax.rem(here_z + dz, Z_HI)
        y = lax.rem(here_y + dy, Y)
        core = lax.rem(here_core + dcore, CORES)
        return z * GROUP + y * CORES + core

    def remote(src, dst, send, recv, device):
        return pltpu.make_async_remote_copy(
            src_ref=src,
            dst_ref=dst,
            send_sem=send,
            recv_sem=recv,
            device_id={"samp": device},
            device_id_type=pl.DeviceIdType.MESH,
        )

    def fill(group, member, into):
        slot = partner(group, member, True)
        prompt = slot_prompt_ref[slot]
        at = group * GROUP + member
        into[at, :query_rows] = query_ref[prompt]
        own = own_ref[prompt]
        into[at, query_rows : query_rows + OWN] = own[:, :head_size]
        into[at, query_rows + OWN :] = own[:, head_size:]

    loads = [
        pltpu.make_async_copy(query_hbm, query_ref, load_sem.at[0]),
        pltpu.make_async_copy(own_hbm, own_rows, load_sem.at[1]),
        pltpu.make_async_copy(cache_hbm, cache_ref, load_sem.at[2]),
    ]
    for load in loads:
        load.start()
    barrier = pltpu.get_barrier_semaphore()

    def greet(at, carry):
        pl.semaphore_signal(
            barrier,
            inc=1,
            device_id={"samp": partner(at // GROUP, lax.rem(at, GROUP), True)},
            device_id_type=pl.DeviceIdType.MESH,
        )
        return carry

    lax.fori_loop(1, prompts, greet, 0)
    loads[1].wait()
    rows = own_rows.shape[0] // prompts
    together = OWN // math.gcd(OWN, rows)
    blank = jnp.zeros((OWN - rows, own_ref.shape[2]), jnp.float32)
    for first in range(0, prompts, together):
        block = own_rows[first * rows : (first + together) * rows].astype(jnp.float32)
        for prompt in range(together):
            piece = jnp.concatenate([block[prompt * rows : (prompt + 1) * rows], blank], axis=0)
            own_ref[first + prompt] = piece.astype(jnp.bfloat16)
    loads[0].wait()
    fill(0, 0, held)

    def prepare(at, carry):
        fill(at // GROUP, lax.rem(at, GROUP), sent)
        return carry

    lax.fori_loop(1, prompts, prepare, 0)

    def send_out(at, carry):
        group = at // GROUP
        remote(
            sent.at[at],
            held.at[at],
            sent_sem,
            held_sem.at[group],
            partner(group, lax.rem(at, GROUP), True),
        ).start()
        return carry

    pl.semaphore_wait(barrier, prompts - 1)
    for group in range(Z_HI):
        lax.fori_loop(max(1, group * GROUP), (group + 1) * GROUP, send_out, 0)

    def find(prompt, carry):
        def look(slot, found):
            return jnp.where(slot_prompt_ref[slot] == prompt, slot, found)

        slot_of[prompt] = lax.fori_loop(0, prompts, look, 0)
        return carry

    lax.fori_loop(0, prompts, find, 0)

    factor = math.log2(math.e) / math.sqrt(head_size)
    nt = (((1,), (1,)), ((), ()))
    nn = (((1,), (0,)), ((), ()))

    def attend(group, first):
        base = group * GROUP
        count = GROUP - 1 if first else GROUP
        start = base + GROUP - count
        arrived = held.at[pl.ds(start, count)]
        pltpu.make_async_copy(arrived, arrived, held_sem.at[group]).wait()
        query = held[pl.ds(base, GROUP), :query_rows].reshape(GROUP * query_rows, head_size)
        key = held[pl.ds(base, GROUP), query_rows : query_rows + OWN]
        key = key.reshape(GROUP * OWN, head_size)
        value = held[pl.ds(base, GROUP), query_rows + OWN :].reshape(GROUP * OWN, head_size)
        prompt_score = lax.dot_general(
            query, cache_ref[:, :head_size], nt, preferred_element_type=jnp.float32
        )
        own_score = lax.dot_general(query, key, nt, preferred_element_type=jnp.float32)
        line = lax.broadcasted_iota(jnp.int32, own_score.shape, 0)
        column = lax.broadcasted_iota(jnp.int32, own_score.shape, 1)
        row = lax.rem(line, query_rows) // heads
        own = lax.rem(column, OWN)
        seen = (line // query_rows == column // OWN) & (own <= row)
        seen = seen & (own >= row - lax.rem(row, STEPS))
        own_score = jnp.where(seen, own_score, -jnp.inf)
        maximum = jnp.maximum(
            jnp.max(prompt_score, -1, keepdims=True), jnp.max(own_score, -1, keepdims=True)
        )
        shift = maximum * factor
        prompt_weight = jnp.exp2(prompt_score * factor - shift)
        own_weight = jnp.exp2(own_score * factor - shift)
        denominator = jnp.sum(prompt_weight, -1, keepdims=True) + jnp.sum(
            own_weight, -1, keepdims=True
        )
        summed = lax.dot_general(
            prompt_weight.astype(jnp.bfloat16),
            cache_ref[:, head_size:],
            nn,
            preferred_element_type=jnp.float32,
        )
        summed = summed + lax.dot_general(
            own_weight.astype(jnp.bfloat16), value, nn, preferred_element_type=jnp.float32
        )
        attended = (summed / denominator).astype(jnp.bfloat16)
        attended = attended.reshape(GROUP, query_rows, head_size)
        done[pl.ds(base, GROUP)] = attended
        if first:
            back[0] = attended[0]

        def send_back(at, carry):
            remote(
                done.at[at],
                back.at[at],
                done_sem,
                back_sem,
                partner(group, at - base, False),
            ).start()
            return carry

        lax.fori_loop(start, base + GROUP, send_back, 0)

    loads[2].wait()
    attend(0, True)

    def attend_next(group, carry):
        attend(group, False)
        return carry

    lax.fori_loop(1, Z_HI, attend_next, 0)
    others = sent.at[pl.ds(1, prompts - 1)]
    pltpu.make_async_copy(others, others, sent_sem).wait()
    others = done.at[pl.ds(1, prompts - 1)]
    pltpu.make_async_copy(others, others, done_sem).wait()
    others = back.at[pl.ds(1, prompts - 1)]
    pltpu.make_async_copy(others, others, back_sem).wait()

    def place(prompt, carry):
        slot = slot_of[prompt]
        dz = lax.rem(slot // GROUP - here_z + Z_HI, Z_HI)
        dy = lax.rem(lax.rem(slot, GROUP) // CORES - here_y + Y, Y)
        dcore = lax.rem(lax.rem(slot, CORES) + here_core, CORES)
        out_ref[prompt] = back[z_distance(dz) * GROUP + dy * CORES + dcore]
        return carry

    lax.fori_loop(0, prompts, place, 0)


def exchange(slot_prompt, query, own_rows, cache, heads):
    prompts, query_rows, head_size = query.shape
    width = query_rows + 2 * OWN
    held = jnp.bfloat16
    dma = pltpu.SemaphoreType.DMA
    hbm = pl.BlockSpec(memory_space=pl.ANY)
    return pl.pallas_call(
        functools.partial(exchange_kernel, heads),
        in_specs=[pl.BlockSpec(memory_space=pltpu.SMEM), hbm, hbm, hbm],
        out_specs=pl.BlockSpec(memory_space=pltpu.VMEM),
        out_shape=jax.ShapeDtypeStruct(query.shape, held),
        scratch_shapes=[
            pltpu.VMEM(query.shape, held),
            pltpu.VMEM((prompts, OWN, 2 * head_size), held),
            pltpu.VMEM(own_rows.shape, held),
            pltpu.VMEM(cache.shape, held),
            pltpu.VMEM((prompts, width, head_size), held),
            pltpu.VMEM((prompts, width, head_size), held),
            pltpu.VMEM(query.shape, held),
            pltpu.VMEM(query.shape, held),
            pltpu.SMEM((prompts,), jnp.int32),
            dma((3,)),
            dma,
            dma((Z_HI,)),
            dma,
            dma,
        ],
        compiler_params=pltpu.CompilerParams(
            collective_id=1, has_side_effects=True, vmem_limit_bytes=60 * 2**20
        ),
    )(slot_prompt, query, own_rows, cache)


RING = 4
RING_UNITS = (2, 2, 2, 2, 1)
PAIR_UNITS = (2, 2, 2, 1)
RING_FIRST = len(RING_UNITS)
PAIR_FIRST = len(PAIR_UNITS)
START_RING, START_PAIR, RING_STEP, RING_END, PAIR_STEP, PAIR_RING = range(6)
ORDER = (
    (START_RING, 4, 0),
    (START_PAIR, 3, 0),
    (START_RING, 2, 0),
    (START_RING, 1, 0),
    (RING_STEP, 4, 0),
    (START_PAIR, 2, 0),
    (PAIR_STEP, 3, 0),
    (START_RING, 0, 0),
    (RING_STEP, 4, 1),
    (START_PAIR, 1, 0),
    (RING_STEP, 1, 0),
    (START_PAIR, 0, 0),
    (PAIR_RING, 3, 0),
    (START_RING, 3, 0),
    (PAIR_STEP, 2, 0),
    (RING_STEP, 0, 0),
    (RING_STEP, 4, 2),
    (RING_STEP, 2, 0),
    (RING_STEP, 1, 1),
    (PAIR_RING, 3, 1),
    (RING_STEP, 3, 0),
    (RING_STEP, 0, 1),
    (PAIR_RING, 2, 0),
    (PAIR_STEP, 1, 0),
    (RING_STEP, 2, 1),
    (RING_STEP, 1, 2),
    (PAIR_RING, 3, 2),
    (RING_STEP, 3, 1),
    (RING_STEP, 0, 2),
    (PAIR_STEP, 0, 0),
    (PAIR_RING, 2, 1),
    (PAIR_RING, 1, 0),
    (RING_STEP, 2, 2),
    (RING_END, 4, 0),
    (RING_END, 1, 0),
    (RING_STEP, 3, 2),
    (RING_END, 0, 0),
    (PAIR_RING, 0, 0),
    (PAIR_RING, 2, 2),
    (PAIR_RING, 1, 1),
    (RING_END, 2, 0),
    (PAIR_RING, 0, 1),
    (RING_END, 3, 0),
    (PAIR_RING, 1, 2),
    (PAIR_RING, 0, 2),
)


def project_kernel(
    attended_ref,
    weight_hbm,
    out_ref,
    weight,
    weight_sem,
    xp,
    xr,
    xq,
    zp,
    zq,
    zr,
    xr_send,
    xr_recv,
    xq_send,
    xq_recv,
    zq_send,
    zq_recv,
    zr_send,
    zr_recv,
):
    rows = out_ref.shape[0]
    here = lax.axis_index("tp")
    x = lax.rem(here, RING)
    z = here // RING
    other = 1 - z

    def ring_device(way):
        step = 1 if way == 0 else RING - 1
        return {"tp": z * RING + lax.rem(x + step, RING)}

    pair_device = {"tp": other * RING + x}

    def block(way, step):
        ahead = 2 * RING - 1 - step if way == 0 else 1 + step
        return lax.rem(x + ahead, RING)

    unit = out_ref.shape[1] // (2 * (sum(RING_UNITS) + sum(PAIR_UNITS)))
    chunks = {}
    start = 0
    for units in (RING_UNITS, PAIR_UNITS):
        for k in range(len(units)):
            for way in range(2):
                chunks[(units is RING_UNITS, k, way)] = (len(chunks), start, units[k] * unit)
                start += units[k] * unit

    def ring_width(k):
        return RING_UNITS[k] * unit

    def pair_width(k):
        return PAIR_UNITS[k] * unit

    def fetch(chunk):
        index, start, width = chunk
        return pltpu.make_async_copy(
            weight_hbm.at[:, pl.ds(start, width)],
            weight.at[index, :, pl.ds(0, width)],
            weight_sem.at[index],
        )

    def remote(src, dst, send, recv, device):
        return pltpu.make_async_remote_copy(
            src_ref=src,
            dst_ref=dst,
            send_sem=send,
            recv_sem=recv,
            device_id=device,
            device_id_type=pl.DeviceIdType.MESH,
        )

    def ring_copy(k, way, step):
        return remote(
            xp.at[way, k, block(way, step), :, :, pl.ds(0, ring_width(k))],
            xr.at[way, k, step, :, :, pl.ds(0, ring_width(k))],
            xr_send.at[way, k, step],
            xr_recv.at[way, k, step],
            ring_device(way),
        )

    def ring_pair_copy(k, way):
        return remote(
            xp.at[way, k, x, other, :, pl.ds(0, ring_width(k))],
            xq.at[way, k, :, pl.ds(0, ring_width(k))],
            xq_send.at[way, k],
            xq_recv.at[way, k],
            pair_device,
        )

    def pair_copy(k, way):
        return remote(
            zp.at[way, k, other, :, :, pl.ds(0, pair_width(k))],
            zq.at[way, k, :, :, pl.ds(0, pair_width(k))],
            zq_send.at[way, k],
            zq_recv.at[way, k],
            pair_device,
        )

    def pair_ring_copy(k, way, step):
        return remote(
            zp.at[way, k, z, block(way, step), :, pl.ds(0, pair_width(k))],
            zr.at[way, k, step, :, pl.ds(0, pair_width(k))],
            zr_send.at[way, k, step],
            zr_recv.at[way, k, step],
            ring_device(way),
        )

    def multiply(chunk):
        fetch(chunk).wait()
        index, _, width = chunk
        product = jnp.dot(
            attended_ref[...], weight[index, :, :width], preferred_element_type=jnp.float32
        )
        return product.astype(jnp.bfloat16)

    def start_ring(k, way):
        product = multiply(chunks[(True, k, way)])
        for j in range(2 * RING):
            part = product[j * rows : (j + 1) * rows]
            xp[way, k, j % RING, j // RING, :, : ring_width(k)] = part
        ring_copy(k, way, 0).start()

    def start_pair(k, way):
        product = multiply(chunks[(False, k, way)])
        for j in range(2 * RING):
            part = product[j * rows : (j + 1) * rows]
            zp[way, k, j // RING, j % RING, :, : pair_width(k)] = part
        pair_copy(k, way).start()

    def wide(value):
        return value.astype(jnp.float32)

    def finish(chunk, total):
        _, start, width = chunk
        out_ref[:, start : start + width] = total.astype(jnp.bfloat16)

    def ring_step(k, way, step):
        ring_copy(k, way, step).wait_recv()
        at = block(way, step + 1)
        width = ring_width(k)
        total = wide(xp[way, k, at, :, :, :width]) + wide(xr[way, k, step, :, :, :width])
        xp[way, k, at, :, :, :width] = total.astype(jnp.bfloat16)
        if step < RING - 2:
            ring_copy(k, way, step + 1).start()
        else:
            ring_pair_copy(k, way).start()

    def ring_end(k, way):
        ring_pair_copy(k, way).wait_recv()
        width = ring_width(k)
        finish(
            chunks[(True, k, way)],
            wide(xp[way, k, x, z, :, :width]) + wide(xq[way, k, :, :width]),
        )

    def pair_step(k, way):
        pair_copy(k, way).wait_recv()
        at = block(way, 0)
        width = pair_width(k)
        total = wide(zp[way, k, z, at, :, :width]) + wide(zq[way, k, at, :, :width])
        zp[way, k, z, at, :, :width] = total.astype(jnp.bfloat16)
        pair_ring_copy(k, way, 0).start()

    def pair_ring_step(k, way, step):
        pair_ring_copy(k, way, step).wait_recv()
        at = block(way, step + 1)
        width = pair_width(k)
        total = wide(zp[way, k, z, at, :, :width]) + wide(zq[way, k, at, :, :width])
        total = total + wide(zr[way, k, step, :, :width])
        if step < RING - 2:
            zp[way, k, z, at, :, :width] = total.astype(jnp.bfloat16)
            pair_ring_copy(k, way, step + 1).start()
        else:
            finish(chunks[(False, k, way)], total)

    for kind, k, _ in ORDER:
        if kind in (START_RING, START_PAIR):
            for way in range(2):
                fetch(chunks[(kind == START_RING, k, way)]).start()
    barrier = pltpu.get_barrier_semaphore()
    for device in (ring_device(0), ring_device(1), pair_device):
        pl.semaphore_signal(
            barrier, inc=1, device_id=device, device_id_type=pl.DeviceIdType.MESH
        )
    pl.semaphore_wait(barrier, 3)

    for kind, k, step in ORDER:
        for way in range(2):
            if kind == START_RING:
                start_ring(k, way)
            elif kind == START_PAIR:
                start_pair(k, way)
            elif kind == RING_STEP:
                ring_step(k, way, step)
            elif kind == RING_END:
                ring_end(k, way)
            elif kind == PAIR_STEP:
                pair_step(k, way)
            else:
                pair_ring_step(k, way, step)
    for way in range(2):
        for k in range(RING_FIRST):
            for step in range(RING - 1):
                ring_copy(k, way, step).wait_send()
            ring_pair_copy(k, way).wait_send()
        for k in range(PAIR_FIRST):
            pair_copy(k, way).wait_send()
            for step in range(RING - 1):
                pair_ring_copy(k, way, step).wait_send()


def project(attended, out_weight):
    total, depth = attended.shape
    columns = out_weight.shape[1]
    rows = total // (2 * RING)
    chunks = 2 * (RING_FIRST + PAIR_FIRST)
    units = 2 * (sum(RING_UNITS) + sum(PAIR_UNITS))
    width = max(RING_UNITS + PAIR_UNITS) * columns // units
    steps = RING - 1
    dma = pltpu.SemaphoreType.DMA
    held = jnp.bfloat16
    return pl.pallas_call(
        project_kernel,
        in_specs=[
            pl.BlockSpec(memory_space=pltpu.VMEM),
            pl.BlockSpec(memory_space=pl.ANY),
        ],
        out_specs=pl.BlockSpec(memory_space=pltpu.VMEM),
        out_shape=jax.ShapeDtypeStruct((rows, columns), held),
        scratch_shapes=[
            pltpu.VMEM((chunks, depth, width), held),
            dma((chunks,)),
            pltpu.VMEM((2, RING_FIRST, RING, 2, rows, width), held),
            pltpu.VMEM((2, RING_FIRST, steps, 2, rows, width), held),
            pltpu.VMEM((2, RING_FIRST, rows, width), held),
            pltpu.VMEM((2, PAIR_FIRST, 2, RING, rows, width), held),
            pltpu.VMEM((2, PAIR_FIRST, RING, rows, width), held),
            pltpu.VMEM((2, PAIR_FIRST, steps, rows, width), held),
            dma((2, RING_FIRST, steps)),
            dma((2, RING_FIRST, steps)),
            dma((2, RING_FIRST)),
            dma((2, RING_FIRST)),
            dma((2, PAIR_FIRST)),
            dma((2, PAIR_FIRST)),
            dma((2, PAIR_FIRST, steps)),
            dma((2, PAIR_FIRST, steps)),
        ],
        compiler_params=pltpu.CompilerParams(
            collective_id=0, has_side_effects=True, vmem_limit_bytes=48 * 2**20
        ),
        cost_estimate=pl.CostEstimate(
            flops=2 * total * depth * columns,
            bytes_accessed=2 * (depth * columns + total * depth + rows * columns),
            transcendentals=0,
        ),
    )(attended, out_weight)


def on_device(queries, cache, new_kv, slot_prompt, residual, out_weight, gain):
    row_total, heads_local, head_size = queries.shape
    prompts = slot_prompt.shape[0]
    rows = row_total // prompts
    attended = exchange(
        slot_prompt,
        queries.reshape(prompts, rows * heads_local, head_size),
        new_kv.reshape(row_total, 2 * head_size),
        cache.reshape(cache.shape[1], 2 * head_size),
        heads_local,
    )
    attended = attended.reshape(row_total, heads_local * head_size)
    projected = project(attended, out_weight).astype(jnp.float32)
    hidden = (residual.astype(jnp.float32) + projected).astype(jnp.bfloat16)
    hidden_f = hidden.astype(jnp.float32)
    spread = jnp.sqrt(jnp.mean(hidden_f * hidden_f, -1) + 1e-05)
    normed = (hidden_f / spread[:, None] * gain[None, :]).astype(jnp.bfloat16)
    return (hidden, normed)


def solution(mesh):
    placed = (
        P("samp", "tp", None),
        P("samp", None, "tp", None),
        P("samp", "tp", None),
        P(),
        P(("samp", "tp"), None),
        P("tp", None),
        P(),
    )
    return jax.shard_map(
        on_device,
        mesh=mesh,
        in_specs=placed,
        out_specs=(P(("samp", "tp"), None), P(("samp", "tp"), None)),
        check_vma=False,
    )
```

```python
import functools
import math

import jax
import jax.numpy as jnp
from jax import lax
from jax.experimental import pallas as pl
from jax.experimental.pallas import tpu as pltpu
from jax.sharding import PartitionSpec as P

STEPS = 3
Z_HI = 4
Y = 4
CORES = 2
GROUP = Y * CORES
OWN = 16
RING = 4
TP_PARTNERS = 3


def exchange(
    heads,
    begin,
    slot_prompt_ref,
    query_hbm,
    own_hbm,
    cache_hbm,
    attended_ref,
    query_ref,
    own_ref,
    own_rows,
    cache_ref,
    sent,
    held,
    done,
    back,
    slot_of,
    load_sem,
    sent_sem,
    held_sem,
    done_sem,
    back_sem,
):
    prompts, query_rows, head_size = query_ref.shape
    width = sent.shape[1]
    here = lax.axis_index("samp")
    here_z = here // GROUP
    here_y = lax.rem(here, GROUP) // CORES
    here_core = lax.rem(here, CORES)

    def z_distance(group):
        return lax.rem(group * (group + 1) // 2, Z_HI)

    def partner(group, member, away):
        dz = z_distance(group)
        dy = member // CORES
        dcore = lax.rem(member, CORES)
        if not away:
            dz = Z_HI - dz
            dy = Y - dy
        z = lax.rem(here_z + dz, Z_HI)
        y = lax.rem(here_y + dy, Y)
        core = lax.rem(here_core + dcore, CORES)
        return z * GROUP + y * CORES + core

    def remote(src, dst, send, recv, device):
        return pltpu.make_async_remote_copy(
            src_ref=src,
            dst_ref=dst,
            send_sem=send,
            recv_sem=recv,
            device_id={"samp": device},
            device_id_type=pl.DeviceIdType.MESH,
        )

    def fill(group, member, into):
        slot = partner(group, member, True)
        prompt = slot_prompt_ref[slot]
        at = group * GROUP + member
        into[at, :query_rows] = query_ref[prompt]
        own = own_ref[prompt]
        into[at, query_rows : query_rows + OWN] = own[:, :head_size]
        into[at, query_rows + OWN :] = own[:, head_size:]

    loads = [
        pltpu.make_async_copy(query_hbm, query_ref, load_sem.at[0]),
        pltpu.make_async_copy(own_hbm, own_rows, load_sem.at[1]),
        pltpu.make_async_copy(cache_hbm, cache_ref, load_sem.at[2]),
    ]
    for load in loads:
        load.start()
    begin()
    barrier = pltpu.get_barrier_semaphore()

    def greet(at, carry):
        pl.semaphore_signal(
            barrier,
            inc=1,
            device_id={"samp": partner(at // GROUP, lax.rem(at, GROUP), True)},
            device_id_type=pl.DeviceIdType.MESH,
        )
        return carry

    lax.fori_loop(1, prompts, greet, 0)
    loads[1].wait()
    rows = own_rows.shape[0] // prompts
    together = OWN // math.gcd(OWN, rows)
    blank = jnp.zeros((OWN - rows, own_ref.shape[2]), jnp.float32)
    for first in range(0, prompts, together):
        block = own_rows[first * rows : (first + together) * rows].astype(jnp.float32)
        for prompt in range(together):
            piece = jnp.concatenate([block[prompt * rows : (prompt + 1) * rows], blank], axis=0)
            own_ref[first + prompt] = piece.astype(jnp.bfloat16)
    loads[0].wait()
    fill(0, 0, held)

    def prepare(at, carry):
        fill(at // GROUP, lax.rem(at, GROUP), sent)
        return carry

    lax.fori_loop(1, prompts, prepare, 0)

    def send_out(at, carry):
        group = at // GROUP
        remote(
            sent.at[at],
            held.at[at],
            sent_sem,
            held_sem.at[group],
            partner(group, lax.rem(at, GROUP), True),
        ).start()
        return carry

    pl.semaphore_wait(barrier, prompts - 1 + TP_PARTNERS)
    for group in range(Z_HI):
        lax.fori_loop(max(1, group * GROUP), (group + 1) * GROUP, send_out, 0)

    def find(prompt, carry):
        def look(slot, found):
            return jnp.where(slot_prompt_ref[slot] == prompt, slot, found)

        slot_of[prompt] = lax.fori_loop(0, prompts, look, 0)
        return carry

    lax.fori_loop(0, prompts, find, 0)

    factor = math.log2(math.e) / math.sqrt(head_size)
    nt = (((1,), (1,)), ((), ()))
    nn = (((1,), (0,)), ((), ()))

    def attend(group, first):
        base = group * GROUP
        count = GROUP - 1 if first else GROUP
        start = base + GROUP - count
        arrived = held.at[pl.ds(start, count)]
        pltpu.make_async_copy(arrived, arrived, held_sem.at[group]).wait()
        query = held[pl.ds(base, GROUP), :query_rows].reshape(GROUP * query_rows, head_size)
        key = held[pl.ds(base, GROUP), query_rows : query_rows + OWN]
        key = key.reshape(GROUP * OWN, head_size)
        value = held[pl.ds(base, GROUP), query_rows + OWN :].reshape(GROUP * OWN, head_size)
        prompt_score = lax.dot_general(
            query, cache_ref[:, :head_size], nt, preferred_element_type=jnp.float32
        )
        own_score = lax.dot_general(query, key, nt, preferred_element_type=jnp.float32)
        line = lax.broadcasted_iota(jnp.int32, own_score.shape, 0)
        column = lax.broadcasted_iota(jnp.int32, own_score.shape, 1)
        row = lax.rem(line, query_rows) // heads
        own = lax.rem(column, OWN)
        seen = (line // query_rows == column // OWN) & (own <= row)
        seen = seen & (own >= row - lax.rem(row, STEPS))
        own_score = jnp.where(seen, own_score, -jnp.inf)
        maximum = jnp.maximum(
            jnp.max(prompt_score, -1, keepdims=True), jnp.max(own_score, -1, keepdims=True)
        )
        shift = maximum * factor
        prompt_weight = jnp.exp2(prompt_score * factor - shift)
        own_weight = jnp.exp2(own_score * factor - shift)
        denominator = jnp.sum(prompt_weight, -1, keepdims=True) + jnp.sum(
            own_weight, -1, keepdims=True
        )
        summed = lax.dot_general(
            prompt_weight.astype(jnp.bfloat16),
            cache_ref[:, head_size:],
            nn,
            preferred_element_type=jnp.float32,
        )
        summed = summed + lax.dot_general(
            own_weight.astype(jnp.bfloat16), value, nn, preferred_element_type=jnp.float32
        )
        attended = (summed / denominator).astype(jnp.bfloat16)
        attended = attended.reshape(GROUP, query_rows, head_size)
        done[pl.ds(base, GROUP)] = attended
        if first:
            back[0] = attended[0]

        def send_back(at, carry):
            remote(
                done.at[at],
                back.at[at],
                done_sem,
                back_sem,
                partner(group, at - base, False),
            ).start()
            return carry

        lax.fori_loop(start, base + GROUP, send_back, 0)

    loads[2].wait()
    attend(0, True)

    def attend_next(group, carry):
        attend(group, False)
        return carry

    lax.fori_loop(1, Z_HI, attend_next, 0)
    others = sent.at[pl.ds(1, prompts - 1)]
    pltpu.make_async_copy(others, others, sent_sem).wait()
    others = done.at[pl.ds(1, prompts - 1)]
    pltpu.make_async_copy(others, others, done_sem).wait()
    others = back.at[pl.ds(1, prompts - 1)]
    pltpu.make_async_copy(others, others, back_sem).wait()

    block_rows = together * rows
    lines = block_rows * heads
    at = lax.broadcasted_iota(jnp.int32, (lines, lines), 0)
    taken = lax.broadcasted_iota(jnp.int32, (lines, lines), 1)
    wanted = lax.rem(at, block_rows) * heads + at // block_rows
    move = jnp.where(taken == wanted, 1.0, 0.0).astype(jnp.bfloat16)

    def arrived_from(slot):
        dz = lax.rem(slot // GROUP - here_z + Z_HI, Z_HI)
        dy = lax.rem(lax.rem(slot, GROUP) // CORES - here_y + Y, Y)
        dcore = lax.rem(lax.rem(slot, CORES) + here_core, CORES)
        return back[z_distance(dz) * GROUP + dy * CORES + dcore]

    def place(block, carry):
        pieces = [arrived_from(slot_of[block * together + j]) for j in range(together)]
        moved = lax.dot_general(
            move, jnp.concatenate(pieces, axis=0), nn, preferred_element_type=jnp.float32
        ).astype(jnp.bfloat16)
        into = pl.ds(pl.multiple_of(block * block_rows, block_rows), block_rows)
        for head in range(heads):
            columns = pl.ds(head * head_size, head_size)
            attended_ref[into, columns] = moved[head * block_rows : (head + 1) * block_rows]
        return carry

    lax.fori_loop(0, prompts // together, place, 0)


RING_UNITS = (2, 2, 2, 2, 1)
PAIR_UNITS = (2, 2, 2, 1)
RING_FIRST = len(RING_UNITS)
PAIR_FIRST = len(PAIR_UNITS)
START_RING, START_PAIR, RING_STEP, RING_END, PAIR_STEP, PAIR_RING = range(6)
ORDER = (
    (START_RING, 4, 0),
    (START_PAIR, 3, 0),
    (START_RING, 2, 0),
    (START_RING, 1, 0),
    (RING_STEP, 4, 0),
    (START_PAIR, 2, 0),
    (PAIR_STEP, 3, 0),
    (START_RING, 0, 0),
    (RING_STEP, 4, 1),
    (START_PAIR, 1, 0),
    (RING_STEP, 1, 0),
    (START_PAIR, 0, 0),
    (PAIR_RING, 3, 0),
    (START_RING, 3, 0),
    (PAIR_STEP, 2, 0),
    (RING_STEP, 0, 0),
    (RING_STEP, 4, 2),
    (RING_STEP, 2, 0),
    (RING_STEP, 1, 1),
    (PAIR_RING, 3, 1),
    (RING_STEP, 3, 0),
    (RING_STEP, 0, 1),
    (PAIR_RING, 2, 0),
    (PAIR_STEP, 1, 0),
    (RING_STEP, 2, 1),
    (RING_STEP, 1, 2),
    (PAIR_RING, 3, 2),
    (RING_STEP, 3, 1),
    (RING_STEP, 0, 2),
    (PAIR_STEP, 0, 0),
    (PAIR_RING, 2, 1),
    (PAIR_RING, 1, 0),
    (RING_STEP, 2, 2),
    (RING_END, 4, 0),
    (RING_END, 1, 0),
    (RING_STEP, 3, 2),
    (RING_END, 0, 0),
    (PAIR_RING, 0, 0),
    (PAIR_RING, 2, 2),
    (PAIR_RING, 1, 1),
    (RING_END, 2, 0),
    (PAIR_RING, 0, 1),
    (RING_END, 3, 0),
    (PAIR_RING, 1, 2),
    (PAIR_RING, 0, 2),
)


def project(
    attended_ref,
    weight_hbm,
    out_ref,
    weight,
    weight_sem,
    xp,
    xr,
    xq,
    zp,
    zq,
    zr,
    xr_send,
    xr_recv,
    xq_send,
    xq_recv,
    zq_send,
    zq_recv,
    zr_send,
    zr_recv,
):
    rows = out_ref.shape[0]
    here = lax.axis_index("tp")
    x = lax.rem(here, RING)
    z = here // RING
    other = 1 - z

    def ring_device(way):
        step = 1 if way == 0 else RING - 1
        return {"tp": z * RING + lax.rem(x + step, RING)}

    pair_device = {"tp": other * RING + x}

    def block(way, step):
        ahead = 2 * RING - 1 - step if way == 0 else 1 + step
        return lax.rem(x + ahead, RING)

    unit = out_ref.shape[1] // (2 * (sum(RING_UNITS) + sum(PAIR_UNITS)))
    chunks = {}
    start = 0
    for units in (RING_UNITS, PAIR_UNITS):
        for k in range(len(units)):
            for way in range(2):
                chunks[(units is RING_UNITS, k, way)] = (len(chunks), start, units[k] * unit)
                start += units[k] * unit

    def ring_width(k):
        return RING_UNITS[k] * unit

    def pair_width(k):
        return PAIR_UNITS[k] * unit

    def fetch(chunk):
        index, start, width = chunk
        return pltpu.make_async_copy(
            weight_hbm.at[:, pl.ds(start, width)],
            weight.at[index, :, pl.ds(0, width)],
            weight_sem.at[index],
        )

    def remote(src, dst, send, recv, device):
        return pltpu.make_async_remote_copy(
            src_ref=src,
            dst_ref=dst,
            send_sem=send,
            recv_sem=recv,
            device_id=device,
            device_id_type=pl.DeviceIdType.MESH,
        )

    def ring_copy(k, way, step):
        return remote(
            xp.at[way, k, block(way, step), :, :, pl.ds(0, ring_width(k))],
            xr.at[way, k, step, :, :, pl.ds(0, ring_width(k))],
            xr_send.at[way, k, step],
            xr_recv.at[way, k, step],
            ring_device(way),
        )

    def ring_pair_copy(k, way):
        return remote(
            xp.at[way, k, x, other, :, pl.ds(0, ring_width(k))],
            xq.at[way, k, :, pl.ds(0, ring_width(k))],
            xq_send.at[way, k],
            xq_recv.at[way, k],
            pair_device,
        )

    def pair_copy(k, way):
        return remote(
            zp.at[way, k, other, :, :, pl.ds(0, pair_width(k))],
            zq.at[way, k, :, :, pl.ds(0, pair_width(k))],
            zq_send.at[way, k],
            zq_recv.at[way, k],
            pair_device,
        )

    def pair_ring_copy(k, way, step):
        return remote(
            zp.at[way, k, z, block(way, step), :, pl.ds(0, pair_width(k))],
            zr.at[way, k, step, :, pl.ds(0, pair_width(k))],
            zr_send.at[way, k, step],
            zr_recv.at[way, k, step],
            ring_device(way),
        )

    def multiply(chunk):
        fetch(chunk).wait()
        index, _, width = chunk
        product = jnp.dot(
            attended_ref[...], weight[index, :, :width], preferred_element_type=jnp.float32
        )
        return product.astype(jnp.bfloat16)

    def start_ring(k, way):
        product = multiply(chunks[(True, k, way)])
        for j in range(2 * RING):
            part = product[j * rows : (j + 1) * rows]
            xp[way, k, j % RING, j // RING, :, : ring_width(k)] = part
        ring_copy(k, way, 0).start()

    def start_pair(k, way):
        product = multiply(chunks[(False, k, way)])
        for j in range(2 * RING):
            part = product[j * rows : (j + 1) * rows]
            zp[way, k, j // RING, j % RING, :, : pair_width(k)] = part
        pair_copy(k, way).start()

    def wide(value):
        return value.astype(jnp.float32)

    def finish(chunk, total):
        _, start, width = chunk
        out_ref[:, start : start + width] = total.astype(jnp.bfloat16)

    def ring_step(k, way, step):
        ring_copy(k, way, step).wait_recv()
        at = block(way, step + 1)
        width = ring_width(k)
        total = wide(xp[way, k, at, :, :, :width]) + wide(xr[way, k, step, :, :, :width])
        xp[way, k, at, :, :, :width] = total.astype(jnp.bfloat16)
        if step < RING - 2:
            ring_copy(k, way, step + 1).start()
        else:
            ring_pair_copy(k, way).start()

    def ring_end(k, way):
        ring_pair_copy(k, way).wait_recv()
        width = ring_width(k)
        finish(
            chunks[(True, k, way)],
            wide(xp[way, k, x, z, :, :width]) + wide(xq[way, k, :, :width]),
        )

    def pair_step(k, way):
        pair_copy(k, way).wait_recv()
        at = block(way, 0)
        width = pair_width(k)
        total = wide(zp[way, k, z, at, :, :width]) + wide(zq[way, k, at, :, :width])
        zp[way, k, z, at, :, :width] = total.astype(jnp.bfloat16)
        pair_ring_copy(k, way, 0).start()

    def pair_ring_step(k, way, step):
        pair_ring_copy(k, way, step).wait_recv()
        at = block(way, step + 1)
        width = pair_width(k)
        total = wide(zp[way, k, z, at, :, :width]) + wide(zq[way, k, at, :, :width])
        total = total + wide(zr[way, k, step, :, :width])
        if step < RING - 2:
            zp[way, k, z, at, :, :width] = total.astype(jnp.bfloat16)
            pair_ring_copy(k, way, step + 1).start()
        else:
            finish(chunks[(False, k, way)], total)

    def begin():
        for kind, k, _ in ORDER:
            if kind in (START_RING, START_PAIR):
                for way in range(2):
                    fetch(chunks[(kind == START_RING, k, way)]).start()
        barrier = pltpu.get_barrier_semaphore()
        for device in (ring_device(0), ring_device(1), pair_device):
            pl.semaphore_signal(
                barrier, inc=1, device_id=device, device_id_type=pl.DeviceIdType.MESH
            )

    def run():
        for kind, k, step in ORDER:
            for way in range(2):
                if kind == START_RING:
                    start_ring(k, way)
                elif kind == START_PAIR:
                    start_pair(k, way)
                elif kind == RING_STEP:
                    ring_step(k, way, step)
                elif kind == RING_END:
                    ring_end(k, way)
                elif kind == PAIR_STEP:
                    pair_step(k, way)
                else:
                    pair_ring_step(k, way, step)
        for way in range(2):
            for k in range(RING_FIRST):
                for step in range(RING - 1):
                    ring_copy(k, way, step).wait_send()
                ring_pair_copy(k, way).wait_send()
            for k in range(PAIR_FIRST):
                pair_copy(k, way).wait_send()
                for step in range(RING - 1):
                    pair_ring_copy(k, way, step).wait_send()

    return begin, run


def kernel(heads, *refs):
    inputs, out_ref, scratch = refs[:5], refs[5], refs[6:]
    slot_prompt_ref, query_hbm, own_hbm, cache_hbm, weight_hbm = inputs
    attended_ref, exchange_scratch, project_scratch = scratch[0], scratch[1:15], scratch[15:]
    begin, run = project(attended_ref, weight_hbm, out_ref, *project_scratch)
    exchange(
        heads,
        begin,
        slot_prompt_ref,
        query_hbm,
        own_hbm,
        cache_hbm,
        attended_ref,
        *exchange_scratch,
    )
    run()


def attend_and_project(slot_prompt, query, own_rows, cache, out_weight, heads):
    prompts, query_rows, head_size = query.shape
    message = query_rows + 2 * OWN
    held = jnp.bfloat16
    dma = pltpu.SemaphoreType.DMA
    hbm = pl.BlockSpec(memory_space=pl.ANY)
    depth, columns = out_weight.shape
    total = own_rows.shape[0]
    rows = total // (2 * RING)
    chunks = 2 * (RING_FIRST + PAIR_FIRST)
    units = 2 * (sum(RING_UNITS) + sum(PAIR_UNITS))
    width = max(RING_UNITS + PAIR_UNITS) * columns // units
    steps = RING - 1
    return pl.pallas_call(
        functools.partial(kernel, heads),
        in_specs=[pl.BlockSpec(memory_space=pltpu.SMEM), hbm, hbm, hbm, hbm],
        out_specs=pl.BlockSpec(memory_space=pltpu.VMEM),
        out_shape=jax.ShapeDtypeStruct((rows, columns), held),
        scratch_shapes=[
            pltpu.VMEM((total, depth), held),
            pltpu.VMEM(query.shape, held),
            pltpu.VMEM((prompts, OWN, 2 * head_size), held),
            pltpu.VMEM(own_rows.shape, held),
            pltpu.VMEM(cache.shape, held),
            pltpu.VMEM((prompts, message, head_size), held),
            pltpu.VMEM((prompts, message, head_size), held),
            pltpu.VMEM(query.shape, held),
            pltpu.VMEM(query.shape, held),
            pltpu.SMEM((prompts,), jnp.int32),
            dma((3,)),
            dma,
            dma((Z_HI,)),
            dma,
            dma,
            pltpu.VMEM((chunks, depth, width), held),
            dma((chunks,)),
            pltpu.VMEM((2, RING_FIRST, RING, 2, rows, width), held),
            pltpu.VMEM((2, RING_FIRST, steps, 2, rows, width), held),
            pltpu.VMEM((2, RING_FIRST, rows, width), held),
            pltpu.VMEM((2, PAIR_FIRST, 2, RING, rows, width), held),
            pltpu.VMEM((2, PAIR_FIRST, RING, rows, width), held),
            pltpu.VMEM((2, PAIR_FIRST, steps, rows, width), held),
            dma((2, RING_FIRST, steps)),
            dma((2, RING_FIRST, steps)),
            dma((2, RING_FIRST)),
            dma((2, RING_FIRST)),
            dma((2, PAIR_FIRST)),
            dma((2, PAIR_FIRST)),
            dma((2, PAIR_FIRST, steps)),
            dma((2, PAIR_FIRST, steps)),
        ],
        compiler_params=pltpu.CompilerParams(
            collective_id=0, has_side_effects=True, vmem_limit_bytes=60 * 2**20
        ),
    )(slot_prompt, query, own_rows, cache, out_weight)


def on_device(queries, cache, new_kv, slot_prompt, residual, out_weight, gain):
    row_total, heads_local, head_size = queries.shape
    prompts = slot_prompt.shape[0]
    rows = row_total // prompts
    projected = attend_and_project(
        slot_prompt,
        queries.reshape(prompts, rows * heads_local, head_size),
        new_kv.reshape(row_total, 2 * head_size),
        cache.reshape(cache.shape[1], 2 * head_size),
        out_weight,
        heads_local,
    ).astype(jnp.float32)
    hidden = (residual.astype(jnp.float32) + projected).astype(jnp.bfloat16)
    hidden_f = hidden.astype(jnp.float32)
    spread = jnp.sqrt(jnp.mean(hidden_f * hidden_f, -1) + 1e-05)
    normed = (hidden_f / spread[:, None] * gain[None, :]).astype(jnp.bfloat16)
    return (hidden, normed)


def solution(mesh):
    placed = (
        P("samp", "tp", None),
        P("samp", None, "tp", None),
        P("samp", "tp", None),
        P(),
        P(("samp", "tp"), None),
        P("tp", None),
        P(),
    )
    return jax.shard_map(
        on_device,
        mesh=mesh,
        in_specs=placed,
        out_specs=(P(("samp", "tp"), None), P(("samp", "tp"), None)),
        check_vma=False,
    )
```

```python
import functools
import math

import jax
import jax.numpy as jnp
from jax import lax
from jax.experimental import pallas as pl
from jax.experimental.pallas import tpu as pltpu
from jax.sharding import PartitionSpec as P

STEPS = 3
Z_HI = 4
Y = 4
CORES = 2
GROUP = Y * CORES
OWN = 16
RING = 4
TP_PARTNERS = 3


def exchange(
    heads,
    begin,
    slot_prompt_ref,
    query_hbm,
    own_hbm,
    cache_hbm,
    attended_ref,
    query_ref,
    own_ref,
    own_rows,
    cache_ref,
    sent,
    held,
    done,
    back,
    offset_of,
    load_sem,
    sent_sem,
    held_sem,
    done_sem,
    back_sem,
):
    prompts, query_rows, head_size = query_ref.shape
    width = sent.shape[1]
    here = lax.axis_index("samp")
    here_z = here // GROUP
    here_y = lax.rem(here, GROUP) // CORES
    here_core = lax.rem(here, CORES)

    def z_distance(group):
        return lax.rem(group * (group + 1) // 2, Z_HI)

    def partner(group, member, away):
        dz = z_distance(group)
        dy = member // CORES
        dcore = lax.rem(member, CORES)
        if not away:
            dz = Z_HI - dz
            dy = Y - dy
        z = lax.rem(here_z + dz, Z_HI)
        y = lax.rem(here_y + dy, Y)
        core = lax.rem(here_core + dcore, CORES)
        return z * GROUP + y * CORES + core

    def remote(src, dst, send, recv, device):
        return pltpu.make_async_remote_copy(
            src_ref=src,
            dst_ref=dst,
            send_sem=send,
            recv_sem=recv,
            device_id={"samp": device},
            device_id_type=pl.DeviceIdType.MESH,
        )

    def fill(group, member, into):
        slot = partner(group, member, True)
        prompt = slot_prompt_ref[slot]
        at = group * GROUP + member
        into[at, :query_rows] = query_ref[prompt]
        own = own_ref[prompt]
        into[at, query_rows : query_rows + OWN] = own[:, :head_size]
        into[at, query_rows + OWN :] = own[:, head_size:]

    loads = [
        pltpu.make_async_copy(query_hbm, query_ref, load_sem.at[0]),
        pltpu.make_async_copy(own_hbm, own_rows, load_sem.at[1]),
        pltpu.make_async_copy(cache_hbm, cache_ref, load_sem.at[2]),
    ]
    for load in loads:
        load.start()
    begin()
    barrier = pltpu.get_barrier_semaphore()

    def greet(at, carry):
        pl.semaphore_signal(
            barrier,
            inc=1,
            device_id={"samp": partner(at // GROUP, lax.rem(at, GROUP), True)},
            device_id_type=pl.DeviceIdType.MESH,
        )
        return carry

    lax.fori_loop(1, prompts, greet, 0)
    loads[1].wait()
    rows = own_rows.shape[0] // prompts
    together = OWN // math.gcd(OWN, rows)
    blank = jnp.zeros((OWN - rows, own_ref.shape[2]), jnp.float32)
    for first in range(0, prompts, together):
        block = own_rows[first * rows : (first + together) * rows].astype(jnp.float32)
        for prompt in range(together):
            piece = jnp.concatenate([block[prompt * rows : (prompt + 1) * rows], blank], axis=0)
            own_ref[first + prompt] = piece.astype(jnp.bfloat16)
    loads[0].wait()
    fill(0, 0, held)

    def prepare(at, carry):
        fill(at // GROUP, lax.rem(at, GROUP), sent)
        return carry

    lax.fori_loop(1, prompts, prepare, 0)

    def send_out(at, carry):
        group = at // GROUP
        remote(
            sent.at[at],
            held.at[at],
            sent_sem,
            held_sem.at[group],
            partner(group, lax.rem(at, GROUP), True),
        ).start()
        return carry

    pl.semaphore_wait(barrier, prompts - 1 + TP_PARTNERS)
    for group in (3, 1, 2, 0):
        lax.fori_loop(max(1, group * GROUP), (group + 1) * GROUP, send_out, 0)

    def find(prompt, carry):
        def look(slot, found):
            return jnp.where(slot_prompt_ref[slot] == prompt, slot, found)

        slot = lax.fori_loop(0, prompts, look, 0)
        dz = lax.rem(slot // GROUP - here_z + Z_HI, Z_HI)
        dy = lax.rem(lax.rem(slot, GROUP) // CORES - here_y + Y, Y)
        dcore = lax.rem(lax.rem(slot, CORES) + here_core, CORES)
        offset_of[prompt] = z_distance(dz) * GROUP + dy * CORES + dcore
        return carry

    lax.fori_loop(0, prompts, find, 0)

    factor = math.log2(math.e) / math.sqrt(head_size)
    nt = (((1,), (1,)), ((), ()))
    nn = (((1,), (0,)), ((), ()))

    def attend(group, first):
        base = group * GROUP
        count = GROUP - 1 if first else GROUP
        start = base + GROUP - count
        arrived = held.at[pl.ds(start, count)]
        pltpu.make_async_copy(arrived, arrived, held_sem.at[group]).wait()
        query = held[pl.ds(base, GROUP), :query_rows].reshape(GROUP * query_rows, head_size)
        key = held[pl.ds(base, GROUP), query_rows : query_rows + OWN]
        key = key.reshape(GROUP * OWN, head_size)
        value = held[pl.ds(base, GROUP), query_rows + OWN :].reshape(GROUP * OWN, head_size)
        prompt_score = lax.dot_general(
            query, cache_ref[:, :head_size], nt, preferred_element_type=jnp.float32
        )
        own_score = lax.dot_general(query, key, nt, preferred_element_type=jnp.float32)
        line = lax.broadcasted_iota(jnp.int32, own_score.shape, 0)
        column = lax.broadcasted_iota(jnp.int32, own_score.shape, 1)
        row = lax.rem(line, query_rows) // heads
        own = lax.rem(column, OWN)
        seen = (line // query_rows == column // OWN) & (own <= row)
        seen = seen & (own >= row - lax.rem(row, STEPS))
        own_score = jnp.where(seen, own_score, -jnp.inf)
        maximum = jnp.maximum(
            jnp.max(prompt_score, -1, keepdims=True), jnp.max(own_score, -1, keepdims=True)
        )
        shift = maximum * factor
        prompt_weight = jnp.exp2(prompt_score * factor - shift)
        own_weight = jnp.exp2(own_score * factor - shift)
        denominator = jnp.sum(prompt_weight, -1, keepdims=True) + jnp.sum(
            own_weight, -1, keepdims=True
        )
        summed = lax.dot_general(
            prompt_weight.astype(jnp.bfloat16),
            cache_ref[:, head_size:],
            nn,
            preferred_element_type=jnp.float32,
        )
        summed = summed + lax.dot_general(
            own_weight.astype(jnp.bfloat16), value, nn, preferred_element_type=jnp.float32
        )
        attended = (summed / denominator).astype(jnp.bfloat16)
        attended = attended.reshape(GROUP, query_rows, head_size)
        done[pl.ds(base, GROUP)] = attended
        if first:
            back[0] = attended[0]

        def send_back(at, carry):
            remote(
                done.at[at],
                back.at[at],
                done_sem,
                back_sem,
                partner(group, at - base, False),
            ).start()
            return carry

        lax.fori_loop(start, base + GROUP, send_back, 0)

    def attend_next(step, carry):
        attend(lax.rem(step + 2, Z_HI - 1) + 1, False)
        return carry

    loads[2].wait()
    lax.fori_loop(0, Z_HI - 1, attend_next, 0)
    attend(0, True)
    others = sent.at[pl.ds(1, prompts - 1)]
    pltpu.make_async_copy(others, others, sent_sem).wait()
    others = done.at[pl.ds(1, prompts - 1)]
    pltpu.make_async_copy(others, others, done_sem).wait()
    others = back.at[pl.ds(1, prompts - 1)]
    pltpu.make_async_copy(others, others, back_sem).wait()

    block_rows = together * rows
    lines = block_rows * heads
    at = lax.broadcasted_iota(jnp.int32, (lines, lines), 0)
    taken = lax.broadcasted_iota(jnp.int32, (lines, lines), 1)
    wanted = lax.rem(at, block_rows) * heads + at // block_rows
    move = jnp.where(taken == wanted, 1.0, 0.0).astype(jnp.bfloat16)

    def place(block, carry):
        pieces = [back[offset_of[block * together + j]] for j in range(together)]
        moved = lax.dot_general(
            move, jnp.concatenate(pieces, axis=0), nn, preferred_element_type=jnp.float32
        ).astype(jnp.bfloat16)
        into = pl.ds(pl.multiple_of(block * block_rows, block_rows), block_rows)
        for head in range(heads):
            columns = pl.ds(head * head_size, head_size)
            attended_ref[into, columns] = moved[head * block_rows : (head + 1) * block_rows]
        return carry

    lax.fori_loop(0, prompts // together, place, 0)


RING_UNITS = (2, 2, 2, 2, 1)
PAIR_UNITS = (2, 2, 2, 1)
RING_FIRST = len(RING_UNITS)
PAIR_FIRST = len(PAIR_UNITS)
START_RING, START_PAIR, RING_STEP, RING_END, PAIR_STEP, PAIR_RING = range(6)
ORDER = (
    (START_RING, 4, 0),
    (START_PAIR, 3, 0),
    (START_RING, 2, 0),
    (START_RING, 1, 0),
    (RING_STEP, 4, 0),
    (START_PAIR, 2, 0),
    (PAIR_STEP, 3, 0),
    (START_RING, 0, 0),
    (RING_STEP, 4, 1),
    (START_PAIR, 1, 0),
    (RING_STEP, 1, 0),
    (START_PAIR, 0, 0),
    (PAIR_RING, 3, 0),
    (START_RING, 3, 0),
    (PAIR_STEP, 2, 0),
    (RING_STEP, 0, 0),
    (RING_STEP, 4, 2),
    (RING_STEP, 2, 0),
    (RING_STEP, 1, 1),
    (PAIR_RING, 3, 1),
    (RING_STEP, 3, 0),
    (RING_STEP, 0, 1),
    (PAIR_RING, 2, 0),
    (PAIR_STEP, 1, 0),
    (RING_STEP, 2, 1),
    (RING_STEP, 1, 2),
    (PAIR_RING, 3, 2),
    (RING_STEP, 3, 1),
    (RING_STEP, 0, 2),
    (PAIR_STEP, 0, 0),
    (PAIR_RING, 2, 1),
    (PAIR_RING, 1, 0),
    (RING_STEP, 2, 2),
    (RING_END, 4, 0),
    (RING_END, 1, 0),
    (RING_STEP, 3, 2),
    (RING_END, 0, 0),
    (PAIR_RING, 0, 0),
    (PAIR_RING, 2, 2),
    (PAIR_RING, 1, 1),
    (RING_END, 2, 0),
    (PAIR_RING, 0, 1),
    (RING_END, 3, 0),
    (PAIR_RING, 1, 2),
    (PAIR_RING, 0, 2),
)


def project(
    attended_ref,
    weight_hbm,
    residual_hbm,
    gain_hbm,
    hidden_ref,
    normed_ref,
    residual,
    gain,
    squares,
    row_sem,
    weight,
    weight_sem,
    xp,
    xr,
    xq,
    zp,
    zq,
    zr,
    xr_send,
    xr_recv,
    xq_send,
    xq_recv,
    zq_send,
    zq_recv,
    zr_send,
    zr_recv,
):
    rows, columns_total = hidden_ref.shape
    here = lax.axis_index("tp")
    x = lax.rem(here, RING)
    z = here // RING
    other = 1 - z

    def ring_device(way):
        step = 1 if way == 0 else RING - 1
        return {"tp": z * RING + lax.rem(x + step, RING)}

    pair_device = {"tp": other * RING + x}

    def block(way, step):
        ahead = 2 * RING - 1 - step if way == 0 else 1 + step
        return lax.rem(x + ahead, RING)

    unit = columns_total // (2 * (sum(RING_UNITS) + sum(PAIR_UNITS)))
    chunks = {}
    start = 0
    for units in (RING_UNITS, PAIR_UNITS):
        for k in range(len(units)):
            for way in range(2):
                chunks[(units is RING_UNITS, k, way)] = (len(chunks), start, units[k] * unit)
                start += units[k] * unit

    def ring_width(k):
        return RING_UNITS[k] * unit

    def pair_width(k):
        return PAIR_UNITS[k] * unit

    def fetch(chunk):
        index, start, width = chunk
        return pltpu.make_async_copy(
            weight_hbm.at[:, pl.ds(start, width)],
            weight.at[index, :, pl.ds(0, width)],
            weight_sem.at[index],
        )

    def remote(src, dst, send, recv, device):
        return pltpu.make_async_remote_copy(
            src_ref=src,
            dst_ref=dst,
            send_sem=send,
            recv_sem=recv,
            device_id=device,
            device_id_type=pl.DeviceIdType.MESH,
        )

    def ring_copy(k, way, step):
        return remote(
            xp.at[way, k, block(way, step), :, :, pl.ds(0, ring_width(k))],
            xr.at[way, k, step, :, :, pl.ds(0, ring_width(k))],
            xr_send.at[way, k, step],
            xr_recv.at[way, k, step],
            ring_device(way),
        )

    def ring_pair_copy(k, way):
        return remote(
            xp.at[way, k, x, other, :, pl.ds(0, ring_width(k))],
            xq.at[way, k, :, pl.ds(0, ring_width(k))],
            xq_send.at[way, k],
            xq_recv.at[way, k],
            pair_device,
        )

    def pair_copy(k, way):
        return remote(
            zp.at[way, k, other, :, :, pl.ds(0, pair_width(k))],
            zq.at[way, k, :, :, pl.ds(0, pair_width(k))],
            zq_send.at[way, k],
            zq_recv.at[way, k],
            pair_device,
        )

    def pair_ring_copy(k, way, step):
        return remote(
            zp.at[way, k, z, block(way, step), :, pl.ds(0, pair_width(k))],
            zr.at[way, k, step, :, pl.ds(0, pair_width(k))],
            zr_send.at[way, k, step],
            zr_recv.at[way, k, step],
            ring_device(way),
        )

    def multiply(chunk):
        fetch(chunk).wait()
        index, _, width = chunk
        product = jnp.dot(
            attended_ref[...], weight[index, :, :width], preferred_element_type=jnp.float32
        )
        return product.astype(jnp.bfloat16)

    def start_ring(k, way):
        product = multiply(chunks[(True, k, way)])
        for j in range(2 * RING):
            part = product[j * rows : (j + 1) * rows]
            xp[way, k, j % RING, j // RING, :, : ring_width(k)] = part
        ring_copy(k, way, 0).start()

    def start_pair(k, way):
        product = multiply(chunks[(False, k, way)])
        for j in range(2 * RING):
            part = product[j * rows : (j + 1) * rows]
            zp[way, k, j // RING, j % RING, :, : pair_width(k)] = part
        pair_copy(k, way).start()

    def wide(value):
        return value.astype(jnp.float32)

    def finish(chunk, total):
        _, start, width = chunk
        columns = slice(start, start + width)
        hidden = (wide(residual[:, columns]) + total).astype(jnp.bfloat16)
        hidden_ref[:, columns] = hidden
        square = wide(hidden) * wide(hidden)
        lanes = squares.shape[1]
        found = squares[...]
        for at in range(0, width, lanes):
            found = found + square[:, at : at + lanes]
        squares[...] = found

    def ring_step(k, way, step):
        ring_copy(k, way, step).wait_recv()
        at = block(way, step + 1)
        width = ring_width(k)
        total = wide(xp[way, k, at, :, :, :width]) + wide(xr[way, k, step, :, :, :width])
        xp[way, k, at, :, :, :width] = total.astype(jnp.bfloat16)
        if step < RING - 2:
            ring_copy(k, way, step + 1).start()
        else:
            ring_pair_copy(k, way).start()

    def ring_end(k, way):
        ring_pair_copy(k, way).wait_recv()
        width = ring_width(k)
        finish(
            chunks[(True, k, way)],
            wide(xp[way, k, x, z, :, :width]) + wide(xq[way, k, :, :width]),
        )

    def pair_step(k, way):
        pair_copy(k, way).wait_recv()
        at = block(way, 0)
        width = pair_width(k)
        total = wide(zp[way, k, z, at, :, :width]) + wide(zq[way, k, at, :, :width])
        zp[way, k, z, at, :, :width] = total.astype(jnp.bfloat16)
        pair_ring_copy(k, way, 0).start()

    def pair_ring_step(k, way, step):
        pair_ring_copy(k, way, step).wait_recv()
        at = block(way, step + 1)
        width = pair_width(k)
        total = wide(zp[way, k, z, at, :, :width]) + wide(zq[way, k, at, :, :width])
        total = total + wide(zr[way, k, step, :, :width])
        if step < RING - 2:
            zp[way, k, z, at, :, :width] = total.astype(jnp.bfloat16)
            pair_ring_copy(k, way, step + 1).start()
        else:
            finish(chunks[(False, k, way)], total)

    row_loads = [
        pltpu.make_async_copy(residual_hbm, residual, row_sem.at[0]),
        pltpu.make_async_copy(gain_hbm, gain, row_sem.at[1]),
    ]

    def begin():
        for kind, k, _ in ORDER:
            if kind in (START_RING, START_PAIR):
                for way in range(2):
                    fetch(chunks[(kind == START_RING, k, way)]).start()
        for load in row_loads:
            load.start()
        barrier = pltpu.get_barrier_semaphore()
        for device in (ring_device(0), ring_device(1), pair_device):
            pl.semaphore_signal(
                barrier, inc=1, device_id=device, device_id_type=pl.DeviceIdType.MESH
            )

    def run():
        for load in row_loads:
            load.wait()
        squares[...] = jnp.zeros_like(squares)
        for kind, k, step in ORDER:
            for way in range(2):
                if kind == START_RING:
                    start_ring(k, way)
                elif kind == START_PAIR:
                    start_pair(k, way)
                elif kind == RING_STEP:
                    ring_step(k, way, step)
                elif kind == RING_END:
                    ring_end(k, way)
                elif kind == PAIR_STEP:
                    pair_step(k, way)
                else:
                    pair_ring_step(k, way, step)
        mean = jnp.sum(squares[...], -1, keepdims=True) / columns_total
        inverse = 1.0 / jnp.sqrt(mean + 1e-05)
        part = 2 * unit
        for at in range(0, columns_total, part):
            columns = slice(at, at + part)
            normed = wide(hidden_ref[:, columns]) * inverse * gain[:, columns]
            normed_ref[:, columns] = normed.astype(jnp.bfloat16)
        for way in range(2):
            for k in range(RING_FIRST):
                for step in range(RING - 1):
                    ring_copy(k, way, step).wait_send()
                ring_pair_copy(k, way).wait_send()
            for k in range(PAIR_FIRST):
                pair_copy(k, way).wait_send()
                for step in range(RING - 1):
                    pair_ring_copy(k, way, step).wait_send()

    return begin, run


def kernel(heads, *refs):
    inputs, outputs, scratch = refs[:7], refs[7:9], refs[9:]
    slot_prompt_ref, query_hbm, own_hbm, cache_hbm = inputs[:4]
    attended_ref, exchange_scratch, project_scratch = scratch[0], scratch[1:15], scratch[15:]
    begin, run = project(attended_ref, *inputs[4:], *outputs, *project_scratch)
    exchange(
        heads,
        begin,
        slot_prompt_ref,
        query_hbm,
        own_hbm,
        cache_hbm,
        attended_ref,
        *exchange_scratch,
    )
    run()


def attend_and_project(slot_prompt, query, own_rows, cache, out_weight, residual, gain, heads):
    prompts, query_rows, head_size = query.shape
    message = query_rows + 2 * OWN
    held = jnp.bfloat16
    dma = pltpu.SemaphoreType.DMA
    hbm = pl.BlockSpec(memory_space=pl.ANY)
    depth, columns = out_weight.shape
    total = own_rows.shape[0]
    rows = total // (2 * RING)
    chunks = 2 * (RING_FIRST + PAIR_FIRST)
    units = 2 * (sum(RING_UNITS) + sum(PAIR_UNITS))
    width = max(RING_UNITS + PAIR_UNITS) * columns // units
    steps = RING - 1
    return pl.pallas_call(
        functools.partial(kernel, heads),
        in_specs=[pl.BlockSpec(memory_space=pltpu.SMEM)] + [hbm] * 6,
        out_specs=[pl.BlockSpec(memory_space=pltpu.VMEM)] * 2,
        out_shape=[jax.ShapeDtypeStruct((rows, columns), held)] * 2,
        scratch_shapes=[
            pltpu.VMEM((total, depth), held),
            pltpu.VMEM(query.shape, held),
            pltpu.VMEM((prompts, OWN, 2 * head_size), held),
            pltpu.VMEM(own_rows.shape, held),
            pltpu.VMEM(cache.shape, held),
            pltpu.VMEM((prompts, message, head_size), held),
            pltpu.VMEM((prompts, message, head_size), held),
            pltpu.VMEM(query.shape, held),
            pltpu.VMEM(query.shape, held),
            pltpu.SMEM((prompts,), jnp.int32),
            dma((3,)),
            dma,
            dma((Z_HI,)),
            dma,
            dma,
            pltpu.VMEM(residual.shape, held),
            pltpu.VMEM(gain.shape, jnp.float32),
            pltpu.VMEM((rows, 128), jnp.float32),
            dma((2,)),
            pltpu.VMEM((chunks, depth, width), held),
            dma((chunks,)),
            pltpu.VMEM((2, RING_FIRST, RING, 2, rows, width), held),
            pltpu.VMEM((2, RING_FIRST, steps, 2, rows, width), held),
            pltpu.VMEM((2, RING_FIRST, rows, width), held),
            pltpu.VMEM((2, PAIR_FIRST, 2, RING, rows, width), held),
            pltpu.VMEM((2, PAIR_FIRST, RING, rows, width), held),
            pltpu.VMEM((2, PAIR_FIRST, steps, rows, width), held),
            dma((2, RING_FIRST, steps)),
            dma((2, RING_FIRST, steps)),
            dma((2, RING_FIRST)),
            dma((2, RING_FIRST)),
            dma((2, PAIR_FIRST)),
            dma((2, PAIR_FIRST)),
            dma((2, PAIR_FIRST, steps)),
            dma((2, PAIR_FIRST, steps)),
        ],
        compiler_params=pltpu.CompilerParams(
            collective_id=0, has_side_effects=True, vmem_limit_bytes=60 * 2**20
        ),
    )(slot_prompt, query, own_rows, cache, out_weight, residual, gain)


def on_device(queries, cache, new_kv, slot_prompt, residual, out_weight, gain):
    row_total, heads_local, head_size = queries.shape
    prompts = slot_prompt.shape[0]
    rows = row_total // prompts
    hidden, normed = attend_and_project(
        slot_prompt,
        queries.reshape(prompts, rows * heads_local, head_size),
        new_kv.reshape(row_total, 2 * head_size),
        cache.reshape(cache.shape[1], 2 * head_size),
        out_weight,
        residual,
        gain[None, :],
        heads_local,
    )
    return (hidden, normed)


def solution(mesh):
    placed = (
        P("samp", "tp", None),
        P("samp", None, "tp", None),
        P("samp", "tp", None),
        P(),
        P(("samp", "tp"), None),
        P("tp", None),
        P(),
    )
    return jax.shard_map(
        on_device,
        mesh=mesh,
        in_specs=placed,
        out_specs=(P(("samp", "tp"), None), P(("samp", "tp"), None)),
        check_vma=False,
    )
```

```python
import functools
import math

import jax
import jax.numpy as jnp
from jax import lax
from jax.experimental import pallas as pl
from jax.experimental.pallas import tpu as pltpu
from jax.sharding import PartitionSpec as P

STEPS = 3
Z_HI = 4
Y = 4
CORES = 2
GROUP = Y * CORES
OWN = 16
RING = 4
TP_PARTNERS = 3


def exchange(
    heads,
    begin,
    slot_prompt_ref,
    query_hbm,
    own_hbm,
    cache_hbm,
    attended_ref,
    query_ref,
    own_ref,
    own_rows,
    cache_ref,
    sent,
    held,
    done,
    back,
    offset_of,
    load_sem,
    sent_sem,
    held_sem,
    done_sem,
    back_sem,
):
    prompts, query_rows, head_size = query_ref.shape
    width = sent.shape[1]
    here = lax.axis_index("samp")
    here_z = here // GROUP
    here_y = lax.rem(here, GROUP) // CORES
    here_core = lax.rem(here, CORES)

    def z_distance(group):
        return lax.rem(group * (group + 1) // 2, Z_HI)

    def partner(group, member, away):
        dz = z_distance(group)
        dy = member // CORES
        dcore = lax.rem(member, CORES)
        if not away:
            dz = Z_HI - dz
            dy = Y - dy
        z = lax.rem(here_z + dz, Z_HI)
        y = lax.rem(here_y + dy, Y)
        core = lax.rem(here_core + dcore, CORES)
        return z * GROUP + y * CORES + core

    def remote(src, dst, send, recv, device):
        return pltpu.make_async_remote_copy(
            src_ref=src,
            dst_ref=dst,
            send_sem=send,
            recv_sem=recv,
            device_id={"samp": device},
            device_id_type=pl.DeviceIdType.MESH,
        )

    def fill(group, member, into):
        slot = partner(group, member, True)
        prompt = slot_prompt_ref[slot]
        at = group * GROUP + member
        into[at, :query_rows] = query_ref[prompt]
        own = own_ref[prompt]
        into[at, query_rows : query_rows + OWN] = own[:, :head_size]
        into[at, query_rows + OWN :] = own[:, head_size:]

    loads = [
        pltpu.make_async_copy(query_hbm, query_ref, load_sem.at[0]),
        pltpu.make_async_copy(own_hbm, own_rows, load_sem.at[1]),
        pltpu.make_async_copy(cache_hbm, cache_ref, load_sem.at[2]),
    ]
    for load in loads:
        load.start()
    begin()
    barrier = pltpu.get_barrier_semaphore()

    def greet(at, carry):
        pl.semaphore_signal(
            barrier,
            inc=1,
            device_id={"samp": partner(at // GROUP, lax.rem(at, GROUP), True)},
            device_id_type=pl.DeviceIdType.MESH,
        )
        return carry

    lax.fori_loop(1, prompts, greet, 0)
    loads[1].wait()
    rows = own_rows.shape[0] // prompts
    together = OWN // math.gcd(OWN, rows)
    blank = jnp.zeros((OWN - rows, own_ref.shape[2]), jnp.float32)
    for first in range(0, prompts, together):
        block = own_rows[first * rows : (first + together) * rows].astype(jnp.float32)
        for prompt in range(together):
            piece = jnp.concatenate([block[prompt * rows : (prompt + 1) * rows], blank], axis=0)
            own_ref[first + prompt] = piece.astype(jnp.bfloat16)
    loads[0].wait()
    fill(0, 0, held)

    def prepare(at, carry):
        fill(at // GROUP, lax.rem(at, GROUP), sent)
        return carry

    lax.fori_loop(1, prompts, prepare, 0)

    def send_out(at, carry):
        group = at // GROUP
        remote(
            sent.at[at],
            held.at[at],
            sent_sem,
            held_sem.at[group],
            partner(group, lax.rem(at, GROUP), True),
        ).start()
        return carry

    pl.semaphore_wait(barrier, prompts - 1 + TP_PARTNERS)
    for group in (3, 1, 2, 0):
        lax.fori_loop(max(1, group * GROUP), (group + 1) * GROUP, send_out, 0)

    def find(prompt, carry):
        def look(slot, found):
            return jnp.where(slot_prompt_ref[slot] == prompt, slot, found)

        slot = lax.fori_loop(0, prompts, look, 0)
        dz = lax.rem(slot // GROUP - here_z + Z_HI, Z_HI)
        dy = lax.rem(lax.rem(slot, GROUP) // CORES - here_y + Y, Y)
        dcore = lax.rem(lax.rem(slot, CORES) + here_core, CORES)
        offset_of[prompt] = z_distance(dz) * GROUP + dy * CORES + dcore
        return carry

    lax.fori_loop(0, prompts, find, 0)

    factor = math.log2(math.e) / math.sqrt(head_size)
    nt = (((1,), (1,)), ((), ()))
    nn = (((1,), (0,)), ((), ()))

    def attend(group, first):
        base = group * GROUP
        count = GROUP - 1 if first else GROUP
        start = base + GROUP - count
        arrived = held.at[pl.ds(start, count)]
        pltpu.make_async_copy(arrived, arrived, held_sem.at[group]).wait()
        query = held[pl.ds(base, GROUP), :query_rows].reshape(GROUP * query_rows, head_size)
        key = held[pl.ds(base, GROUP), query_rows : query_rows + OWN]
        key = key.reshape(GROUP * OWN, head_size)
        value = held[pl.ds(base, GROUP), query_rows + OWN :].reshape(GROUP * OWN, head_size)
        prompt_score = lax.dot_general(
            query, cache_ref[:, :head_size], nt, preferred_element_type=jnp.float32
        )
        own_score = lax.dot_general(query, key, nt, preferred_element_type=jnp.float32)
        line = lax.broadcasted_iota(jnp.int32, own_score.shape, 0)
        column = lax.broadcasted_iota(jnp.int32, own_score.shape, 1)
        row = lax.rem(line, query_rows) // heads
        own = lax.rem(column, OWN)
        seen = (line // query_rows == column // OWN) & (own <= row)
        seen = seen & (own >= row - lax.rem(row, STEPS))
        own_score = jnp.where(seen, own_score, -jnp.inf)
        maximum = jnp.maximum(
            jnp.max(prompt_score, -1, keepdims=True), jnp.max(own_score, -1, keepdims=True)
        )
        shift = maximum * factor
        prompt_weight = jnp.exp2(prompt_score * factor - shift)
        own_weight = jnp.exp2(own_score * factor - shift)
        denominator = jnp.sum(prompt_weight, -1, keepdims=True) + jnp.sum(
            own_weight, -1, keepdims=True
        )
        summed = lax.dot_general(
            prompt_weight.astype(jnp.bfloat16),
            cache_ref[:, head_size:],
            nn,
            preferred_element_type=jnp.float32,
        )
        summed = summed + lax.dot_general(
            own_weight.astype(jnp.bfloat16), value, nn, preferred_element_type=jnp.float32
        )
        attended = (summed / denominator).astype(jnp.bfloat16)
        attended = attended.reshape(GROUP, query_rows, head_size)
        done[pl.ds(base, GROUP)] = attended
        if first:
            back[0] = attended[0]

        def send_back(at, carry):
            remote(
                done.at[at],
                back.at[at],
                done_sem,
                back_sem,
                partner(group, at - base, False),
            ).start()
            return carry

        lax.fori_loop(start, base + GROUP, send_back, 0)

    def attend_next(step, carry):
        attend(lax.rem(step + 2, Z_HI - 1) + 1, False)
        return carry

    loads[2].wait()
    lax.fori_loop(0, Z_HI - 1, attend_next, 0)
    attend(0, True)
    others = sent.at[pl.ds(1, prompts - 1)]
    pltpu.make_async_copy(others, others, sent_sem).wait()
    others = done.at[pl.ds(1, prompts - 1)]
    pltpu.make_async_copy(others, others, done_sem).wait()
    others = back.at[pl.ds(1, prompts - 1)]
    pltpu.make_async_copy(others, others, back_sem).wait()

    block_rows = together * rows
    lines = block_rows * heads
    at = lax.broadcasted_iota(jnp.int32, (lines, lines), 0)
    taken = lax.broadcasted_iota(jnp.int32, (lines, lines), 1)
    wanted = lax.rem(at, block_rows) * heads + at // block_rows
    move = jnp.where(taken == wanted, 1.0, 0.0).astype(jnp.bfloat16)

    def place(block, carry):
        pieces = [back[offset_of[block * together + j]] for j in range(together)]
        moved = lax.dot_general(
            move, jnp.concatenate(pieces, axis=0), nn, preferred_element_type=jnp.float32
        ).astype(jnp.bfloat16)
        into = pl.ds(pl.multiple_of(block * block_rows, block_rows), block_rows)
        for head in range(heads):
            columns = pl.ds(head * head_size, head_size)
            attended_ref[into, columns] = moved[head * block_rows : (head + 1) * block_rows]
        return carry

    lax.fori_loop(0, prompts // together, place, 0)


RING_UNITS = (2, 2, 2, 2, 1)
PAIR_UNITS = (2, 2, 2, 1)
RING_FIRST = len(RING_UNITS)
PAIR_FIRST = len(PAIR_UNITS)
START_RING, START_PAIR, RING_STEP, RING_END, PAIR_STEP, PAIR_RING = range(6)
ORDER = (
    (START_RING, 4, 0),
    (START_PAIR, 3, 0),
    (START_RING, 2, 0),
    (START_RING, 1, 0),
    (RING_STEP, 4, 0),
    (START_PAIR, 2, 0),
    (PAIR_STEP, 3, 0),
    (START_RING, 0, 0),
    (RING_STEP, 4, 1),
    (START_PAIR, 1, 0),
    (RING_STEP, 1, 0),
    (START_PAIR, 0, 0),
    (PAIR_RING, 3, 0),
    (START_RING, 3, 0),
    (PAIR_STEP, 2, 0),
    (RING_STEP, 0, 0),
    (RING_STEP, 4, 2),
    (RING_STEP, 2, 0),
    (RING_STEP, 1, 1),
    (PAIR_RING, 3, 1),
    (RING_STEP, 3, 0),
    (RING_STEP, 0, 1),
    (PAIR_RING, 2, 0),
    (PAIR_STEP, 1, 0),
    (RING_STEP, 2, 1),
    (RING_STEP, 1, 2),
    (PAIR_RING, 3, 2),
    (RING_STEP, 3, 1),
    (RING_STEP, 0, 2),
    (PAIR_STEP, 0, 0),
    (PAIR_RING, 2, 1),
    (PAIR_RING, 1, 0),
    (RING_STEP, 2, 2),
    (RING_END, 4, 0),
    (RING_END, 1, 0),
    (RING_STEP, 3, 2),
    (RING_END, 0, 0),
    (PAIR_RING, 0, 0),
    (PAIR_RING, 2, 2),
    (PAIR_RING, 1, 1),
    (RING_END, 2, 0),
    (PAIR_RING, 0, 1),
    (RING_END, 3, 0),
    (PAIR_RING, 1, 2),
    (PAIR_RING, 0, 2),
)


def project(
    attended_ref,
    weight_hbm,
    residual_hbm,
    projected_ref,
    inverse_ref,
    residual,
    squares,
    row_sem,
    weight,
    weight_sem,
    xp,
    xr,
    xq,
    zp,
    zq,
    zr,
    xr_send,
    xr_recv,
    xq_send,
    xq_recv,
    zq_send,
    zq_recv,
    zr_send,
    zr_recv,
):
    rows, columns_total = projected_ref.shape
    here = lax.axis_index("tp")
    x = lax.rem(here, RING)
    z = here // RING
    other = 1 - z

    def ring_device(way):
        step = 1 if way == 0 else RING - 1
        return {"tp": z * RING + lax.rem(x + step, RING)}

    pair_device = {"tp": other * RING + x}

    def block(way, step):
        ahead = 2 * RING - 1 - step if way == 0 else 1 + step
        return lax.rem(x + ahead, RING)

    unit = columns_total // (2 * (sum(RING_UNITS) + sum(PAIR_UNITS)))
    chunks = {}
    start = 0
    for units in (RING_UNITS, PAIR_UNITS):
        for k in range(len(units)):
            for way in range(2):
                chunks[(units is RING_UNITS, k, way)] = (len(chunks), start, units[k] * unit)
                start += units[k] * unit

    def ring_width(k):
        return RING_UNITS[k] * unit

    def pair_width(k):
        return PAIR_UNITS[k] * unit

    def fetch(chunk):
        index, start, width = chunk
        return pltpu.make_async_copy(
            weight_hbm.at[:, pl.ds(start, width)],
            weight.at[index, :, pl.ds(0, width)],
            weight_sem.at[index],
        )

    def remote(src, dst, send, recv, device):
        return pltpu.make_async_remote_copy(
            src_ref=src,
            dst_ref=dst,
            send_sem=send,
            recv_sem=recv,
            device_id=device,
            device_id_type=pl.DeviceIdType.MESH,
        )

    def ring_copy(k, way, step):
        return remote(
            xp.at[way, k, block(way, step), :, :, pl.ds(0, ring_width(k))],
            xr.at[way, k, step, :, :, pl.ds(0, ring_width(k))],
            xr_send.at[way, k, step],
            xr_recv.at[way, k, step],
            ring_device(way),
        )

    def ring_pair_copy(k, way):
        return remote(
            xp.at[way, k, x, other, :, pl.ds(0, ring_width(k))],
            xq.at[way, k, :, pl.ds(0, ring_width(k))],
            xq_send.at[way, k],
            xq_recv.at[way, k],
            pair_device,
        )

    def pair_copy(k, way):
        return remote(
            zp.at[way, k, other, :, :, pl.ds(0, pair_width(k))],
            zq.at[way, k, :, :, pl.ds(0, pair_width(k))],
            zq_send.at[way, k],
            zq_recv.at[way, k],
            pair_device,
        )

    def pair_ring_copy(k, way, step):
        return remote(
            zp.at[way, k, z, block(way, step), :, pl.ds(0, pair_width(k))],
            zr.at[way, k, step, :, pl.ds(0, pair_width(k))],
            zr_send.at[way, k, step],
            zr_recv.at[way, k, step],
            ring_device(way),
        )

    def multiply(chunk):
        fetch(chunk).wait()
        index, _, width = chunk
        product = jnp.dot(
            attended_ref[...], weight[index, :, :width], preferred_element_type=jnp.float32
        )
        return product.astype(jnp.bfloat16)

    def start_ring(k, way):
        product = multiply(chunks[(True, k, way)])
        for j in range(2 * RING):
            part = product[j * rows : (j + 1) * rows]
            xp[way, k, j % RING, j // RING, :, : ring_width(k)] = part
        ring_copy(k, way, 0).start()

    def start_pair(k, way):
        product = multiply(chunks[(False, k, way)])
        for j in range(2 * RING):
            part = product[j * rows : (j + 1) * rows]
            zp[way, k, j // RING, j % RING, :, : pair_width(k)] = part
        pair_copy(k, way).start()

    def wide(value):
        return value.astype(jnp.float32)

    def finish(chunk, total):
        _, start, width = chunk
        columns = slice(start, start + width)
        projected = total.astype(jnp.bfloat16)
        projected_ref[:, columns] = projected
        hidden = (wide(residual[:, columns]) + wide(projected)).astype(jnp.bfloat16)
        square = wide(hidden) * wide(hidden)
        lanes = squares.shape[1]
        found = squares[...]
        for at in range(0, width, lanes):
            found = found + square[:, at : at + lanes]
        squares[...] = found

    def ring_step(k, way, step):
        ring_copy(k, way, step).wait_recv()
        at = block(way, step + 1)
        width = ring_width(k)
        total = wide(xp[way, k, at, :, :, :width]) + wide(xr[way, k, step, :, :, :width])
        xp[way, k, at, :, :, :width] = total.astype(jnp.bfloat16)
        if step < RING - 2:
            ring_copy(k, way, step + 1).start()
        else:
            ring_pair_copy(k, way).start()

    def ring_end(k, way):
        ring_pair_copy(k, way).wait_recv()
        width = ring_width(k)
        finish(
            chunks[(True, k, way)],
            wide(xp[way, k, x, z, :, :width]) + wide(xq[way, k, :, :width]),
        )

    def pair_step(k, way):
        pair_copy(k, way).wait_recv()
        at = block(way, 0)
        width = pair_width(k)
        total = wide(zp[way, k, z, at, :, :width]) + wide(zq[way, k, at, :, :width])
        zp[way, k, z, at, :, :width] = total.astype(jnp.bfloat16)
        pair_ring_copy(k, way, 0).start()

    def pair_ring_step(k, way, step):
        pair_ring_copy(k, way, step).wait_recv()
        at = block(way, step + 1)
        width = pair_width(k)
        total = wide(zp[way, k, z, at, :, :width]) + wide(zq[way, k, at, :, :width])
        total = total + wide(zr[way, k, step, :, :width])
        if step < RING - 2:
            zp[way, k, z, at, :, :width] = total.astype(jnp.bfloat16)
            pair_ring_copy(k, way, step + 1).start()
        else:
            finish(chunks[(False, k, way)], total)

    row_load = pltpu.make_async_copy(residual_hbm, residual, row_sem)

    def begin():
        for kind, k, _ in ORDER:
            if kind in (START_RING, START_PAIR):
                for way in range(2):
                    fetch(chunks[(kind == START_RING, k, way)]).start()
        row_load.start()
        barrier = pltpu.get_barrier_semaphore()
        for device in (ring_device(0), ring_device(1), pair_device):
            pl.semaphore_signal(
                barrier, inc=1, device_id=device, device_id_type=pl.DeviceIdType.MESH
            )

    def run():
        row_load.wait()
        squares[...] = jnp.zeros_like(squares)
        for kind, k, step in ORDER:
            for way in range(2):
                if kind == START_RING:
                    start_ring(k, way)
                elif kind == START_PAIR:
                    start_pair(k, way)
                elif kind == RING_STEP:
                    ring_step(k, way, step)
                elif kind == RING_END:
                    ring_end(k, way)
                elif kind == PAIR_STEP:
                    pair_step(k, way)
                else:
                    pair_ring_step(k, way, step)
        mean = jnp.sum(squares[...], -1, keepdims=True) / columns_total
        inverse_ref[...] = jnp.broadcast_to(1.0 / jnp.sqrt(mean + 1e-05), inverse_ref.shape)
        for way in range(2):
            for k in range(RING_FIRST):
                for step in range(RING - 1):
                    ring_copy(k, way, step).wait_send()
                ring_pair_copy(k, way).wait_send()
            for k in range(PAIR_FIRST):
                pair_copy(k, way).wait_send()
                for step in range(RING - 1):
                    pair_ring_copy(k, way, step).wait_send()

    return begin, run


def kernel(heads, *refs):
    inputs, outputs, scratch = refs[:6], refs[6:8], refs[8:]
    slot_prompt_ref, query_hbm, own_hbm, cache_hbm = inputs[:4]
    attended_ref, exchange_scratch, project_scratch = scratch[0], scratch[1:15], scratch[15:]
    begin, run = project(attended_ref, *inputs[4:], *outputs, *project_scratch)
    exchange(
        heads,
        begin,
        slot_prompt_ref,
        query_hbm,
        own_hbm,
        cache_hbm,
        attended_ref,
        *exchange_scratch,
    )
    run()


def attend_and_project(slot_prompt, query, own_rows, cache, out_weight, residual, heads):
    prompts, query_rows, head_size = query.shape
    message = query_rows + 2 * OWN
    held = jnp.bfloat16
    dma = pltpu.SemaphoreType.DMA
    hbm = pl.BlockSpec(memory_space=pl.ANY)
    depth, columns = out_weight.shape
    total = own_rows.shape[0]
    rows = total // (2 * RING)
    chunks = 2 * (RING_FIRST + PAIR_FIRST)
    units = 2 * (sum(RING_UNITS) + sum(PAIR_UNITS))
    width = max(RING_UNITS + PAIR_UNITS) * columns // units
    steps = RING - 1
    return pl.pallas_call(
        functools.partial(kernel, heads),
        in_specs=[pl.BlockSpec(memory_space=pltpu.SMEM)] + [hbm] * 5,
        out_specs=[pl.BlockSpec(memory_space=pltpu.VMEM)] * 2,
        out_shape=[
            jax.ShapeDtypeStruct((rows, columns), held),
            jax.ShapeDtypeStruct((rows, 128), jnp.float32),
        ],
        scratch_shapes=[
            pltpu.VMEM((total, depth), held),
            pltpu.VMEM(query.shape, held),
            pltpu.VMEM((prompts, OWN, 2 * head_size), held),
            pltpu.VMEM(own_rows.shape, held),
            pltpu.VMEM(cache.shape, held),
            pltpu.VMEM((prompts, message, head_size), held),
            pltpu.VMEM((prompts, message, head_size), held),
            pltpu.VMEM(query.shape, held),
            pltpu.VMEM(query.shape, held),
            pltpu.SMEM((prompts,), jnp.int32),
            dma((3,)),
            dma,
            dma((Z_HI,)),
            dma,
            dma,
            pltpu.VMEM(residual.shape, held),
            pltpu.VMEM((rows, 128), jnp.float32),
            dma,
            pltpu.VMEM((chunks, depth, width), held),
            dma((chunks,)),
            pltpu.VMEM((2, RING_FIRST, RING, 2, rows, width), held),
            pltpu.VMEM((2, RING_FIRST, steps, 2, rows, width), held),
            pltpu.VMEM((2, RING_FIRST, rows, width), held),
            pltpu.VMEM((2, PAIR_FIRST, 2, RING, rows, width), held),
            pltpu.VMEM((2, PAIR_FIRST, RING, rows, width), held),
            pltpu.VMEM((2, PAIR_FIRST, steps, rows, width), held),
            dma((2, RING_FIRST, steps)),
            dma((2, RING_FIRST, steps)),
            dma((2, RING_FIRST)),
            dma((2, RING_FIRST)),
            dma((2, PAIR_FIRST)),
            dma((2, PAIR_FIRST)),
            dma((2, PAIR_FIRST, steps)),
            dma((2, PAIR_FIRST, steps)),
        ],
        compiler_params=pltpu.CompilerParams(
            collective_id=0, has_side_effects=True, vmem_limit_bytes=60 * 2**20
        ),
    )(slot_prompt, query, own_rows, cache, out_weight, residual)


def on_device(queries, cache, new_kv, slot_prompt, residual, out_weight, gain):
    row_total, heads_local, head_size = queries.shape
    prompts = slot_prompt.shape[0]
    rows = row_total // prompts
    projected, inverse = attend_and_project(
        slot_prompt,
        queries.reshape(prompts, rows * heads_local, head_size),
        new_kv.reshape(row_total, 2 * head_size),
        cache.reshape(cache.shape[1], 2 * head_size),
        out_weight,
        residual,
        heads_local,
    )
    hidden = residual.astype(jnp.float32) + projected.astype(jnp.float32)
    hidden = hidden.astype(jnp.bfloat16)
    normed = hidden.astype(jnp.float32) * inverse[:, :1] * gain[None, :]
    return (hidden, normed.astype(jnp.bfloat16))


def solution(mesh):
    placed = (
        P("samp", "tp", None),
        P("samp", None, "tp", None),
        P("samp", "tp", None),
        P(),
        P(("samp", "tp"), None),
        P("tp", None),
        P(),
    )
    return jax.shard_map(
        on_device,
        mesh=mesh,
        in_specs=placed,
        out_specs=(P(("samp", "tp"), None), P(("samp", "tp"), None)),
        check_vma=False,
    )
```

```python
import functools
import math

import jax
import jax.numpy as jnp
from jax import lax
from jax.experimental import pallas as pl
from jax.experimental.pallas import tpu as pltpu
from jax.sharding import PartitionSpec as P

STEPS = 3
Z_HI = 4
Y = 4
CORES = 2
GROUP = Y * CORES
OWN = 16
RING = 4
TP_PARTNERS = 3


def exchange(
    heads,
    begin,
    slot_prompt_ref,
    query_hbm,
    own_hbm,
    cache_hbm,
    attended_ref,
    query_ref,
    own_ref,
    own_rows,
    cache_ref,
    sent,
    held,
    done,
    back,
    offset_of,
    load_sem,
    sent_sem,
    held_sem,
    done_sem,
    back_sem,
):
    prompts, query_rows, head_size = query_ref.shape
    width = sent.shape[1]
    here = lax.axis_index("samp")
    here_z = here // GROUP
    here_y = lax.rem(here, GROUP) // CORES
    here_core = lax.rem(here, CORES)

    def z_distance(group):
        return lax.rem(group * (group + 1) // 2, Z_HI)

    def partner(group, member, away):
        dz = z_distance(group)
        dy = member // CORES
        dcore = lax.rem(member, CORES)
        if not away:
            dz = Z_HI - dz
            dy = Y - dy
        z = lax.rem(here_z + dz, Z_HI)
        y = lax.rem(here_y + dy, Y)
        core = lax.rem(here_core + dcore, CORES)
        return z * GROUP + y * CORES + core

    def remote(src, dst, send, recv, device):
        return pltpu.make_async_remote_copy(
            src_ref=src,
            dst_ref=dst,
            send_sem=send,
            recv_sem=recv,
            device_id={"samp": device},
            device_id_type=pl.DeviceIdType.MESH,
        )

    def fill(group, member, into):
        slot = partner(group, member, True)
        prompt = slot_prompt_ref[slot]
        at = group * GROUP + member
        into[at, :query_rows] = query_ref[prompt]
        own = own_ref[prompt]
        into[at, query_rows : query_rows + OWN] = own[:, :head_size]
        into[at, query_rows + OWN :] = own[:, head_size:]

    loads = [
        pltpu.make_async_copy(query_hbm, query_ref, load_sem.at[0]),
        pltpu.make_async_copy(own_hbm, own_rows, load_sem.at[1]),
        pltpu.make_async_copy(cache_hbm, cache_ref, load_sem.at[2]),
    ]
    for load in loads:
        load.start()
    begin()
    barrier = pltpu.get_barrier_semaphore()

    def greet(at, carry):
        pl.semaphore_signal(
            barrier,
            inc=1,
            device_id={"samp": partner(at // GROUP, lax.rem(at, GROUP), True)},
            device_id_type=pl.DeviceIdType.MESH,
        )
        return carry

    lax.fori_loop(1, prompts, greet, 0)
    loads[1].wait()
    rows = own_rows.shape[0] // prompts
    together = OWN // math.gcd(OWN, rows)
    blank = jnp.zeros((OWN - rows, own_ref.shape[2]), jnp.float32)
    for first in range(0, prompts, together):
        block = own_rows[first * rows : (first + together) * rows].astype(jnp.float32)
        for prompt in range(together):
            piece = jnp.concatenate([block[prompt * rows : (prompt + 1) * rows], blank], axis=0)
            own_ref[first + prompt] = piece.astype(jnp.bfloat16)
    loads[0].wait()
    fill(0, 0, held)

    def prepare(at, carry):
        fill(at // GROUP, lax.rem(at, GROUP), sent)
        return carry

    lax.fori_loop(1, prompts, prepare, 0)

    def send_out(at, carry):
        group = at // GROUP
        remote(
            sent.at[at],
            held.at[at],
            sent_sem,
            held_sem.at[group],
            partner(group, lax.rem(at, GROUP), True),
        ).start()
        return carry

    pl.semaphore_wait(barrier, prompts - 1 + TP_PARTNERS)
    for group in (3, 1, 2, 0):
        lax.fori_loop(max(1, group * GROUP), (group + 1) * GROUP, send_out, 0)

    def find(prompt, carry):
        def look(slot, found):
            return jnp.where(slot_prompt_ref[slot] == prompt, slot, found)

        slot = lax.fori_loop(0, prompts, look, 0)
        dz = lax.rem(slot // GROUP - here_z + Z_HI, Z_HI)
        dy = lax.rem(lax.rem(slot, GROUP) // CORES - here_y + Y, Y)
        dcore = lax.rem(lax.rem(slot, CORES) + here_core, CORES)
        offset_of[prompt] = z_distance(dz) * GROUP + dy * CORES + dcore
        return carry

    lax.fori_loop(0, prompts, find, 0)

    factor = math.log2(math.e) / math.sqrt(head_size)
    nt = (((1,), (1,)), ((), ()))
    nn = (((1,), (0,)), ((), ()))

    def attend(group, first):
        base = group * GROUP
        count = GROUP - 1 if first else GROUP
        start = base + GROUP - count
        arrived = held.at[pl.ds(start, count)]
        pltpu.make_async_copy(arrived, arrived, held_sem.at[group]).wait()
        query = held[pl.ds(base, GROUP), :query_rows].reshape(GROUP * query_rows, head_size)
        key = held[pl.ds(base, GROUP), query_rows : query_rows + OWN]
        key = key.reshape(GROUP * OWN, head_size)
        value = held[pl.ds(base, GROUP), query_rows + OWN :].reshape(GROUP * OWN, head_size)
        prompt_score = lax.dot_general(
            query, cache_ref[:, :head_size], nt, preferred_element_type=jnp.float32
        )
        own_score = lax.dot_general(query, key, nt, preferred_element_type=jnp.float32)
        line = lax.broadcasted_iota(jnp.int32, own_score.shape, 0)
        column = lax.broadcasted_iota(jnp.int32, own_score.shape, 1)
        row = lax.rem(line, query_rows) // heads
        own = lax.rem(column, OWN)
        seen = (line // query_rows == column // OWN) & (own <= row)
        seen = seen & (own >= row - lax.rem(row, STEPS))
        own_score = jnp.where(seen, own_score, -jnp.inf)
        maximum = jnp.maximum(
            jnp.max(prompt_score, -1, keepdims=True), jnp.max(own_score, -1, keepdims=True)
        )
        shift = maximum * factor
        prompt_weight = jnp.exp2(prompt_score * factor - shift)
        own_weight = jnp.exp2(own_score * factor - shift)
        denominator = jnp.sum(prompt_weight, -1, keepdims=True) + jnp.sum(
            own_weight, -1, keepdims=True
        )
        summed = lax.dot_general(
            prompt_weight.astype(jnp.bfloat16),
            cache_ref[:, head_size:],
            nn,
            preferred_element_type=jnp.float32,
        )
        summed = summed + lax.dot_general(
            own_weight.astype(jnp.bfloat16), value, nn, preferred_element_type=jnp.float32
        )
        attended = (summed / denominator).astype(jnp.bfloat16)
        attended = attended.reshape(GROUP, query_rows, head_size)
        done[pl.ds(base, GROUP)] = attended
        if first:
            back[0] = attended[0]

        def send_back(at, carry):
            remote(
                done.at[at],
                back.at[at],
                done_sem,
                back_sem,
                partner(group, at - base, False),
            ).start()
            return carry

        lax.fori_loop(start, base + GROUP, send_back, 0)

    def attend_next(step, carry):
        attend(lax.rem(step + 2, Z_HI - 1) + 1, False)
        return carry

    loads[2].wait()
    lax.fori_loop(0, Z_HI - 1, attend_next, 0)
    attend(0, True)
    others = sent.at[pl.ds(1, prompts - 1)]
    pltpu.make_async_copy(others, others, sent_sem).wait()
    others = done.at[pl.ds(1, prompts - 1)]
    pltpu.make_async_copy(others, others, done_sem).wait()
    others = back.at[pl.ds(1, prompts - 1)]
    pltpu.make_async_copy(others, others, back_sem).wait()

    block_rows = together * rows
    lines = block_rows * heads
    at = lax.broadcasted_iota(jnp.int32, (lines, lines), 0)
    taken = lax.broadcasted_iota(jnp.int32, (lines, lines), 1)
    wanted = lax.rem(at, block_rows) * heads + at // block_rows
    move = jnp.where(taken == wanted, 1.0, 0.0).astype(jnp.bfloat16)

    def place(block, carry):
        pieces = [back[offset_of[block * together + j]] for j in range(together)]
        moved = lax.dot_general(
            move, jnp.concatenate(pieces, axis=0), nn, preferred_element_type=jnp.float32
        ).astype(jnp.bfloat16)
        into = pl.ds(pl.multiple_of(block * block_rows, block_rows), block_rows)
        for head in range(heads):
            columns = pl.ds(head * head_size, head_size)
            attended_ref[into, columns] = moved[head * block_rows : (head + 1) * block_rows]
        return carry

    lax.fori_loop(0, prompts // together, place, 0)


RING_UNITS = (2, 2, 2, 2, 1)
PAIR_UNITS = (2, 2, 2, 1)
RING_FIRST = len(RING_UNITS)
PAIR_FIRST = len(PAIR_UNITS)
START_RING, START_PAIR, RING_STEP, RING_END, PAIR_STEP, PAIR_RING = range(6)
ORDER = (
    (START_RING, 4, 0),
    (START_RING, 1, 0),
    (START_PAIR, 3, 0),
    (START_RING, 3, 0),
    (START_PAIR, 0, 0),
    (START_PAIR, 1, 0),
    (RING_STEP, 1, 0),
    (PAIR_STEP, 3, 0),
    (START_RING, 0, 0),
    (RING_STEP, 4, 0),
    (RING_STEP, 3, 0),
    (RING_STEP, 1, 1),
    (PAIR_RING, 3, 0),
    (START_PAIR, 2, 0),
    (START_RING, 2, 0),
    (RING_STEP, 0, 0),
    (PAIR_STEP, 0, 0),
    (RING_STEP, 4, 1),
    (RING_STEP, 3, 1),
    (RING_STEP, 1, 2),
    (PAIR_RING, 3, 1),
    (RING_STEP, 0, 1),
    (RING_STEP, 2, 0),
    (PAIR_STEP, 1, 0),
    (RING_STEP, 4, 2),
    (PAIR_RING, 0, 0),
    (RING_STEP, 3, 2),
    (PAIR_RING, 3, 2),
    (RING_STEP, 0, 2),
    (RING_STEP, 2, 1),
    (PAIR_STEP, 2, 0),
    (PAIR_RING, 1, 0),
    (PAIR_RING, 0, 1),
    (RING_END, 1, 0),
    (RING_STEP, 2, 2),
    (RING_END, 4, 0),
    (PAIR_RING, 2, 0),
    (PAIR_RING, 1, 1),
    (RING_END, 3, 0),
    (PAIR_RING, 0, 2),
    (PAIR_RING, 2, 1),
    (RING_END, 0, 0),
    (PAIR_RING, 1, 2),
    (RING_END, 2, 0),
    (PAIR_RING, 2, 2),
)


def project(
    attended_ref,
    weight_hbm,
    out_ref,
    weight,
    weight_sem,
    xp,
    xr,
    xq,
    zp,
    zq,
    zr,
    xr_send,
    xr_recv,
    xq_send,
    xq_recv,
    zq_send,
    zq_recv,
    zr_send,
    zr_recv,
):
    rows = out_ref.shape[0]
    here = lax.axis_index("tp")
    x = lax.rem(here, RING)
    z = here // RING
    other = 1 - z

    def ring_device(way):
        step = 1 if way == 0 else RING - 1
        return {"tp": z * RING + lax.rem(x + step, RING)}

    pair_device = {"tp": other * RING + x}

    def block(way, step):
        ahead = 2 * RING - 1 - step if way == 0 else 1 + step
        return lax.rem(x + ahead, RING)

    unit = out_ref.shape[1] // (2 * (sum(RING_UNITS) + sum(PAIR_UNITS)))
    chunks = {}
    start = 0
    for units in (RING_UNITS, PAIR_UNITS):
        for k in range(len(units)):
            for way in range(2):
                chunks[(units is RING_UNITS, k, way)] = (len(chunks), start, units[k] * unit)
                start += units[k] * unit

    def ring_width(k):
        return RING_UNITS[k] * unit

    def pair_width(k):
        return PAIR_UNITS[k] * unit

    def fetch(chunk):
        index, start, width = chunk
        return pltpu.make_async_copy(
            weight_hbm.at[:, pl.ds(start, width)],
            weight.at[index, :, pl.ds(0, width)],
            weight_sem.at[index],
        )

    def remote(src, dst, send, recv, device):
        return pltpu.make_async_remote_copy(
            src_ref=src,
            dst_ref=dst,
            send_sem=send,
            recv_sem=recv,
            device_id=device,
            device_id_type=pl.DeviceIdType.MESH,
        )

    def ring_copy(k, way, step):
        return remote(
            xp.at[way, k, block(way, step), :, :, pl.ds(0, ring_width(k))],
            xr.at[way, k, step, :, :, pl.ds(0, ring_width(k))],
            xr_send.at[way, k, step],
            xr_recv.at[way, k, step],
            ring_device(way),
        )

    def ring_pair_copy(k, way):
        return remote(
            xp.at[way, k, x, other, :, pl.ds(0, ring_width(k))],
            xq.at[way, k, :, pl.ds(0, ring_width(k))],
            xq_send.at[way, k],
            xq_recv.at[way, k],
            pair_device,
        )

    def pair_copy(k, way):
        return remote(
            zp.at[way, k, other, :, :, pl.ds(0, pair_width(k))],
            zq.at[way, k, :, :, pl.ds(0, pair_width(k))],
            zq_send.at[way, k],
            zq_recv.at[way, k],
            pair_device,
        )

    def pair_ring_copy(k, way, step):
        return remote(
            zp.at[way, k, z, block(way, step), :, pl.ds(0, pair_width(k))],
            zr.at[way, k, step, :, pl.ds(0, pair_width(k))],
            zr_send.at[way, k, step],
            zr_recv.at[way, k, step],
            ring_device(way),
        )

    def multiply(chunk):
        fetch(chunk).wait()
        index, _, width = chunk
        product = jnp.dot(
            attended_ref[...], weight[index, :, :width], preferred_element_type=jnp.float32
        )
        return product.astype(jnp.bfloat16)

    def start_ring(k, way):
        product = multiply(chunks[(True, k, way)])
        for j in range(2 * RING):
            part = product[j * rows : (j + 1) * rows]
            xp[way, k, j % RING, j // RING, :, : ring_width(k)] = part
        ring_copy(k, way, 0).start()

    def start_pair(k, way):
        product = multiply(chunks[(False, k, way)])
        for j in range(2 * RING):
            part = product[j * rows : (j + 1) * rows]
            zp[way, k, j // RING, j % RING, :, : pair_width(k)] = part
        pair_copy(k, way).start()

    def wide(value):
        return value.astype(jnp.float32)

    def finish(chunk, total):
        _, start, width = chunk
        out_ref[:, start : start + width] = total.astype(jnp.bfloat16)

    def ring_step(k, way, step):
        ring_copy(k, way, step).wait_recv()
        at = block(way, step + 1)
        width = ring_width(k)
        total = wide(xp[way, k, at, :, :, :width]) + wide(xr[way, k, step, :, :, :width])
        xp[way, k, at, :, :, :width] = total.astype(jnp.bfloat16)
        if step < RING - 2:
            ring_copy(k, way, step + 1).start()
        else:
            ring_pair_copy(k, way).start()

    def ring_end(k, way):
        ring_pair_copy(k, way).wait_recv()
        width = ring_width(k)
        finish(
            chunks[(True, k, way)],
            wide(xp[way, k, x, z, :, :width]) + wide(xq[way, k, :, :width]),
        )

    def pair_step(k, way):
        pair_copy(k, way).wait_recv()
        at = block(way, 0)
        width = pair_width(k)
        total = wide(zp[way, k, z, at, :, :width]) + wide(zq[way, k, at, :, :width])
        zp[way, k, z, at, :, :width] = total.astype(jnp.bfloat16)
        pair_ring_copy(k, way, 0).start()

    def pair_ring_step(k, way, step):
        pair_ring_copy(k, way, step).wait_recv()
        at = block(way, step + 1)
        width = pair_width(k)
        total = wide(zp[way, k, z, at, :, :width]) + wide(zq[way, k, at, :, :width])
        total = total + wide(zr[way, k, step, :, :width])
        if step < RING - 2:
            zp[way, k, z, at, :, :width] = total.astype(jnp.bfloat16)
            pair_ring_copy(k, way, step + 1).start()
        else:
            finish(chunks[(False, k, way)], total)

    def begin():
        for kind, k, _ in ORDER:
            if kind in (START_RING, START_PAIR):
                for way in range(2):
                    fetch(chunks[(kind == START_RING, k, way)]).start()
        barrier = pltpu.get_barrier_semaphore()
        for device in (ring_device(0), ring_device(1), pair_device):
            pl.semaphore_signal(
                barrier, inc=1, device_id=device, device_id_type=pl.DeviceIdType.MESH
            )

    def run():
        for kind, k, step in ORDER:
            for way in range(2):
                if kind == START_RING:
                    start_ring(k, way)
                elif kind == START_PAIR:
                    start_pair(k, way)
                elif kind == RING_STEP:
                    ring_step(k, way, step)
                elif kind == RING_END:
                    ring_end(k, way)
                elif kind == PAIR_STEP:
                    pair_step(k, way)
                else:
                    pair_ring_step(k, way, step)
        for way in range(2):
            for k in range(RING_FIRST):
                for step in range(RING - 1):
                    ring_copy(k, way, step).wait_send()
                ring_pair_copy(k, way).wait_send()
            for k in range(PAIR_FIRST):
                pair_copy(k, way).wait_send()
                for step in range(RING - 1):
                    pair_ring_copy(k, way, step).wait_send()

    return begin, run


def kernel(heads, *refs):
    inputs, out_ref, scratch = refs[:5], refs[5], refs[6:]
    slot_prompt_ref, query_hbm, own_hbm, cache_hbm, weight_hbm = inputs
    attended_ref, exchange_scratch, project_scratch = scratch[0], scratch[1:15], scratch[15:]
    begin, run = project(attended_ref, weight_hbm, out_ref, *project_scratch)
    exchange(
        heads,
        begin,
        slot_prompt_ref,
        query_hbm,
        own_hbm,
        cache_hbm,
        attended_ref,
        *exchange_scratch,
    )
    run()


def attend_and_project(slot_prompt, query, own_rows, cache, out_weight, heads):
    prompts, query_rows, head_size = query.shape
    message = query_rows + 2 * OWN
    held = jnp.bfloat16
    dma = pltpu.SemaphoreType.DMA
    hbm = pl.BlockSpec(memory_space=pl.ANY)
    depth, columns = out_weight.shape
    total = own_rows.shape[0]
    rows = total // (2 * RING)
    chunks = 2 * (RING_FIRST + PAIR_FIRST)
    units = 2 * (sum(RING_UNITS) + sum(PAIR_UNITS))
    width = max(RING_UNITS + PAIR_UNITS) * columns // units
    steps = RING - 1
    return pl.pallas_call(
        functools.partial(kernel, heads),
        in_specs=[pl.BlockSpec(memory_space=pltpu.SMEM), hbm, hbm, hbm, hbm],
        out_specs=pl.BlockSpec(memory_space=pltpu.VMEM),
        out_shape=jax.ShapeDtypeStruct((rows, columns), held),
        scratch_shapes=[
            pltpu.VMEM((total, depth), held),
            pltpu.VMEM(query.shape, held),
            pltpu.VMEM((prompts, OWN, 2 * head_size), held),
            pltpu.VMEM(own_rows.shape, held),
            pltpu.VMEM(cache.shape, held),
            pltpu.VMEM((prompts, message, head_size), held),
            pltpu.VMEM((prompts, message, head_size), held),
            pltpu.VMEM(query.shape, held),
            pltpu.VMEM(query.shape, held),
            pltpu.SMEM((prompts,), jnp.int32),
            dma((3,)),
            dma,
            dma((Z_HI,)),
            dma,
            dma,
            pltpu.VMEM((chunks, depth, width), held),
            dma((chunks,)),
            pltpu.VMEM((2, RING_FIRST, RING, 2, rows, width), held),
            pltpu.VMEM((2, RING_FIRST, steps, 2, rows, width), held),
            pltpu.VMEM((2, RING_FIRST, rows, width), held),
            pltpu.VMEM((2, PAIR_FIRST, 2, RING, rows, width), held),
            pltpu.VMEM((2, PAIR_FIRST, RING, rows, width), held),
            pltpu.VMEM((2, PAIR_FIRST, steps, rows, width), held),
            dma((2, RING_FIRST, steps)),
            dma((2, RING_FIRST, steps)),
            dma((2, RING_FIRST)),
            dma((2, RING_FIRST)),
            dma((2, PAIR_FIRST)),
            dma((2, PAIR_FIRST)),
            dma((2, PAIR_FIRST, steps)),
            dma((2, PAIR_FIRST, steps)),
        ],
        compiler_params=pltpu.CompilerParams(
            collective_id=0, has_side_effects=True, vmem_limit_bytes=60 * 2**20
        ),
    )(slot_prompt, query, own_rows, cache, out_weight)


def on_device(queries, cache, new_kv, slot_prompt, residual, out_weight, gain):
    row_total, heads_local, head_size = queries.shape
    prompts = slot_prompt.shape[0]
    rows = row_total // prompts
    projected = attend_and_project(
        slot_prompt,
        queries.reshape(prompts, rows * heads_local, head_size),
        new_kv.reshape(row_total, 2 * head_size),
        cache.reshape(cache.shape[1], 2 * head_size),
        out_weight,
        heads_local,
    ).astype(jnp.float32)
    hidden = (residual.astype(jnp.float32) + projected).astype(jnp.bfloat16)
    hidden_f = hidden.astype(jnp.float32)
    spread = jnp.sqrt(jnp.mean(hidden_f * hidden_f, -1) + 1e-05)
    normed = (hidden_f / spread[:, None] * gain[None, :]).astype(jnp.bfloat16)
    return (hidden, normed)


def solution(mesh):
    placed = (
        P("samp", "tp", None),
        P("samp", None, "tp", None),
        P("samp", "tp", None),
        P(),
        P(("samp", "tp"), None),
        P("tp", None),
        P(),
    )
    return jax.shard_map(
        on_device,
        mesh=mesh,
        in_specs=placed,
        out_specs=(P(("samp", "tp"), None), P(("samp", "tp"), None)),
        check_vma=False,
    )
```

```python
import functools
import math

import jax
import jax.numpy as jnp
from jax import lax
from jax.experimental import pallas as pl
from jax.experimental.pallas import tpu as pltpu
from jax.sharding import PartitionSpec as P

STEPS = 3
Z_HI = 4
Y = 4
CORES = 2
GROUP = Y * CORES
OWN = 16
RING = 4
TP_PARTNERS = 3


def exchange(
    heads,
    begin,
    slot_prompt_ref,
    query_hbm,
    own_hbm,
    cache_hbm,
    attended_ref,
    query_ref,
    own_ref,
    own_rows,
    cache_ref,
    sent,
    held,
    done,
    back,
    offset_of,
    load_sem,
    sent_sem,
    held_sem,
    done_sem,
    back_sem,
):
    prompts, query_rows, head_size = query_ref.shape
    width = sent.shape[1]
    here = lax.axis_index("samp")
    here_z = here // GROUP
    here_y = lax.rem(here, GROUP) // CORES
    here_core = lax.rem(here, CORES)

    def z_distance(group):
        return lax.rem(group * (group + 1) // 2, Z_HI)

    def partner(group, member, away):
        dz = z_distance(group)
        dy = member // CORES
        dcore = lax.rem(member, CORES)
        if not away:
            dz = Z_HI - dz
            dy = Y - dy
        z = lax.rem(here_z + dz, Z_HI)
        y = lax.rem(here_y + dy, Y)
        core = lax.rem(here_core + dcore, CORES)
        return z * GROUP + y * CORES + core

    def remote(src, dst, send, recv, device):
        return pltpu.make_async_remote_copy(
            src_ref=src,
            dst_ref=dst,
            send_sem=send,
            recv_sem=recv,
            device_id={"samp": device},
            device_id_type=pl.DeviceIdType.MESH,
        )

    def fill(group, member, into):
        slot = partner(group, member, True)
        prompt = slot_prompt_ref[slot]
        at = group * GROUP + member
        into[at, :query_rows] = query_ref[prompt]
        own = own_ref[prompt]
        into[at, query_rows : query_rows + OWN] = own[:, :head_size]
        into[at, query_rows + OWN :] = own[:, head_size:]

    loads = [
        pltpu.make_async_copy(query_hbm, query_ref, load_sem.at[0]),
        pltpu.make_async_copy(own_hbm, own_rows, load_sem.at[1]),
        pltpu.make_async_copy(cache_hbm, cache_ref, load_sem.at[2]),
    ]
    for load in loads:
        load.start()
    begin()
    barrier = pltpu.get_barrier_semaphore()

    def greet(at, carry):
        pl.semaphore_signal(
            barrier,
            inc=1,
            device_id={"samp": partner(at // GROUP, lax.rem(at, GROUP), True)},
            device_id_type=pl.DeviceIdType.MESH,
        )
        return carry

    lax.fori_loop(1, prompts, greet, 0)
    loads[1].wait()
    rows = own_rows.shape[0] // prompts
    together = OWN // math.gcd(OWN, rows)
    blank = jnp.zeros((OWN - rows, own_ref.shape[2]), jnp.float32)
    for first in range(0, prompts, together):
        block = own_rows[first * rows : (first + together) * rows].astype(jnp.float32)
        for prompt in range(together):
            piece = jnp.concatenate([block[prompt * rows : (prompt + 1) * rows], blank], axis=0)
            own_ref[first + prompt] = piece.astype(jnp.bfloat16)
    loads[0].wait()
    fill(0, 0, held)

    def prepare(at, carry):
        fill(at // GROUP, lax.rem(at, GROUP), sent)
        return carry

    lax.fori_loop(1, prompts, prepare, 0)

    def send_out(at, carry):
        group = at // GROUP
        remote(
            sent.at[at],
            held.at[at],
            sent_sem,
            held_sem.at[group],
            partner(group, lax.rem(at, GROUP), True),
        ).start()
        return carry

    pl.semaphore_wait(barrier, prompts - 1 + TP_PARTNERS)
    for group in (3, 1, 2, 0):
        lax.fori_loop(max(1, group * GROUP), (group + 1) * GROUP, send_out, 0)

    def find(prompt, carry):
        def look(slot, found):
            return jnp.where(slot_prompt_ref[slot] == prompt, slot, found)

        slot = lax.fori_loop(0, prompts, look, 0)
        dz = lax.rem(slot // GROUP - here_z + Z_HI, Z_HI)
        dy = lax.rem(lax.rem(slot, GROUP) // CORES - here_y + Y, Y)
        dcore = lax.rem(lax.rem(slot, CORES) + here_core, CORES)
        offset_of[prompt] = z_distance(dz) * GROUP + dy * CORES + dcore
        return carry

    lax.fori_loop(0, prompts, find, 0)

    factor = math.log2(math.e) / math.sqrt(head_size)
    nt = (((1,), (1,)), ((), ()))
    nn = (((1,), (0,)), ((), ()))

    def attend(group, first):
        base = group * GROUP
        count = GROUP - 1 if first else GROUP
        start = base + GROUP - count
        arrived = held.at[pl.ds(start, count)]
        pltpu.make_async_copy(arrived, arrived, held_sem.at[group]).wait()
        query = held[pl.ds(base, GROUP), :query_rows].reshape(GROUP * query_rows, head_size)
        key = held[pl.ds(base, GROUP), query_rows : query_rows + OWN]
        key = key.reshape(GROUP * OWN, head_size)
        value = held[pl.ds(base, GROUP), query_rows + OWN :].reshape(GROUP * OWN, head_size)
        prompt_score = lax.dot_general(
            query, cache_ref[:, :head_size], nt, preferred_element_type=jnp.float32
        )
        own_score = lax.dot_general(query, key, nt, preferred_element_type=jnp.float32)
        line = lax.broadcasted_iota(jnp.int32, own_score.shape, 0)
        column = lax.broadcasted_iota(jnp.int32, own_score.shape, 1)
        row = lax.rem(line, query_rows) // heads
        own = lax.rem(column, OWN)
        seen = (line // query_rows == column // OWN) & (own <= row)
        seen = seen & (own >= row - lax.rem(row, STEPS))
        own_score = jnp.where(seen, own_score, -jnp.inf)
        maximum = jnp.maximum(
            jnp.max(prompt_score, -1, keepdims=True), jnp.max(own_score, -1, keepdims=True)
        )
        shift = maximum * factor
        prompt_weight = jnp.exp2(prompt_score * factor - shift)
        own_weight = jnp.exp2(own_score * factor - shift)
        denominator = jnp.sum(prompt_weight, -1, keepdims=True) + jnp.sum(
            own_weight, -1, keepdims=True
        )
        summed = lax.dot_general(
            prompt_weight.astype(jnp.bfloat16),
            cache_ref[:, head_size:],
            nn,
            preferred_element_type=jnp.float32,
        )
        summed = summed + lax.dot_general(
            own_weight.astype(jnp.bfloat16), value, nn, preferred_element_type=jnp.float32
        )
        attended = (summed / denominator).astype(jnp.bfloat16)
        attended = attended.reshape(GROUP, query_rows, head_size)
        done[pl.ds(base, GROUP)] = attended
        if first:
            back[0] = attended[0]

        def send_back(at, carry):
            remote(
                done.at[at],
                back.at[at],
                done_sem,
                back_sem,
                partner(group, at - base, False),
            ).start()
            return carry

        lax.fori_loop(start, base + GROUP, send_back, 0)

    def attend_next(step, carry):
        attend(lax.rem(step + 2, Z_HI - 1) + 1, False)
        return carry

    loads[2].wait()
    lax.fori_loop(0, Z_HI - 1, attend_next, 0)
    attend(0, True)
    others = sent.at[pl.ds(1, prompts - 1)]
    pltpu.make_async_copy(others, others, sent_sem).wait()
    others = done.at[pl.ds(1, prompts - 1)]
    pltpu.make_async_copy(others, others, done_sem).wait()
    others = back.at[pl.ds(1, prompts - 1)]
    pltpu.make_async_copy(others, others, back_sem).wait()

    block_rows = together * rows
    lines = block_rows * heads
    at = lax.broadcasted_iota(jnp.int32, (lines, lines), 0)
    taken = lax.broadcasted_iota(jnp.int32, (lines, lines), 1)
    wanted = lax.rem(at, block_rows) * heads + at // block_rows
    move = jnp.where(taken == wanted, 1.0, 0.0).astype(jnp.bfloat16)

    def place(block, carry):
        pieces = [back[offset_of[block * together + j]] for j in range(together)]
        moved = lax.dot_general(
            move, jnp.concatenate(pieces, axis=0), nn, preferred_element_type=jnp.float32
        ).astype(jnp.bfloat16)
        into = pl.ds(pl.multiple_of(block * block_rows, block_rows), block_rows)
        for head in range(heads):
            columns = pl.ds(head * head_size, head_size)
            attended_ref[into, columns] = moved[head * block_rows : (head + 1) * block_rows]
        return carry

    lax.fori_loop(0, prompts // together, place, 0)


RING_UNITS = (2, 2, 2, 2, 1)
PAIR_UNITS = (2, 2, 2, 1)
RING_FIRST = len(RING_UNITS)
PAIR_FIRST = len(PAIR_UNITS)
START_RING, START_PAIR, RING_STEP, RING_END, PAIR_STEP, PAIR_RING = range(6)
ORDER = (
    (START_RING, 4, 0),
    (START_RING, 3, 0),
    (START_PAIR, 3, 0),
    (START_RING, 0, 0),
    (RING_STEP, 4, 0),
    (START_PAIR, 2, 0),
    (START_RING, 2, 0),
    (PAIR_STEP, 3, 0),
    (RING_STEP, 3, 0),
    (RING_STEP, 0, 0),
    (RING_STEP, 4, 1),
    (START_PAIR, 1, 0),
    (START_RING, 1, 0),
    (RING_STEP, 2, 0),
    (PAIR_RING, 3, 0),
    (START_PAIR, 0, 0),
    (PAIR_STEP, 2, 0),
    (RING_STEP, 3, 1),
    (RING_STEP, 0, 1),
    (RING_STEP, 4, 2),
    (RING_STEP, 1, 0),
    (RING_STEP, 2, 1),
    (PAIR_STEP, 1, 0),
    (PAIR_RING, 3, 1),
    (PAIR_RING, 2, 0),
    (RING_STEP, 3, 2),
    (RING_STEP, 0, 2),
    (RING_STEP, 1, 1),
    (RING_STEP, 2, 2),
    (PAIR_STEP, 0, 0),
    (PAIR_RING, 1, 0),
    (PAIR_RING, 3, 2),
    (PAIR_RING, 2, 1),
    (RING_END, 4, 0),
    (RING_STEP, 1, 2),
    (RING_END, 3, 0),
    (PAIR_RING, 0, 0),
    (PAIR_RING, 1, 1),
    (RING_END, 0, 0),
    (PAIR_RING, 2, 2),
    (PAIR_RING, 0, 1),
    (RING_END, 2, 0),
    (PAIR_RING, 1, 2),
    (RING_END, 1, 0),
    (PAIR_RING, 0, 2),
)


def project(
    attended_ref,
    weight_hbm,
    out_ref,
    weight,
    weight_sem,
    xp,
    xr,
    xq,
    zp,
    zq,
    zr,
    xr_send,
    xr_recv,
    xq_send,
    xq_recv,
    zq_send,
    zq_recv,
    zr_send,
    zr_recv,
):
    rows = out_ref.shape[0]
    here = lax.axis_index("tp")
    x = lax.rem(here, RING)
    z = here // RING
    other = 1 - z

    def ring_device(way):
        step = 1 if way == 0 else RING - 1
        return {"tp": z * RING + lax.rem(x + step, RING)}

    pair_device = {"tp": other * RING + x}

    def block(way, step):
        ahead = 2 * RING - 1 - step if way == 0 else 1 + step
        return lax.rem(x + ahead, RING)

    unit = out_ref.shape[1] // (2 * (sum(RING_UNITS) + sum(PAIR_UNITS)))
    chunks = {}
    start = 0
    for units in (RING_UNITS, PAIR_UNITS):
        for k in range(len(units)):
            for way in range(2):
                chunks[(units is RING_UNITS, k, way)] = (len(chunks), start, units[k] * unit)
                start += units[k] * unit

    def ring_width(k):
        return RING_UNITS[k] * unit

    def pair_width(k):
        return PAIR_UNITS[k] * unit

    def fetch(chunk):
        index, start, width = chunk
        return pltpu.make_async_copy(
            weight_hbm.at[:, pl.ds(start, width)],
            weight.at[index, :, pl.ds(0, width)],
            weight_sem.at[index],
        )

    def remote(src, dst, send, recv, device):
        return pltpu.make_async_remote_copy(
            src_ref=src,
            dst_ref=dst,
            send_sem=send,
            recv_sem=recv,
            device_id=device,
            device_id_type=pl.DeviceIdType.MESH,
        )

    def ring_copy(k, way, step):
        return remote(
            xp.at[way, k, block(way, step), :, :, pl.ds(0, ring_width(k))],
            xr.at[way, k, step, :, :, pl.ds(0, ring_width(k))],
            xr_send.at[way, k, step],
            xr_recv.at[way, k, step],
            ring_device(way),
        )

    def ring_pair_copy(k, way):
        return remote(
            xp.at[way, k, x, other, :, pl.ds(0, ring_width(k))],
            xq.at[way, k, :, pl.ds(0, ring_width(k))],
            xq_send.at[way, k],
            xq_recv.at[way, k],
            pair_device,
        )

    def pair_copy(k, way):
        return remote(
            zp.at[way, k, other, :, :, pl.ds(0, pair_width(k))],
            zq.at[way, k, :, :, pl.ds(0, pair_width(k))],
            zq_send.at[way, k],
            zq_recv.at[way, k],
            pair_device,
        )

    def pair_ring_copy(k, way, step):
        return remote(
            zp.at[way, k, z, block(way, step), :, pl.ds(0, pair_width(k))],
            zr.at[way, k, step, :, pl.ds(0, pair_width(k))],
            zr_send.at[way, k, step],
            zr_recv.at[way, k, step],
            ring_device(way),
        )

    def multiply(chunk):
        fetch(chunk).wait()
        index, _, width = chunk
        product = jnp.dot(
            attended_ref[...], weight[index, :, :width], preferred_element_type=jnp.float32
        )
        return product.astype(jnp.bfloat16)

    def start_ring(k, way):
        product = multiply(chunks[(True, k, way)])
        for j in range(2 * RING):
            part = product[j * rows : (j + 1) * rows]
            xp[way, k, j % RING, j // RING, :, : ring_width(k)] = part
        ring_copy(k, way, 0).start()

    def start_pair(k, way):
        product = multiply(chunks[(False, k, way)])
        for j in range(2 * RING):
            part = product[j * rows : (j + 1) * rows]
            zp[way, k, j // RING, j % RING, :, : pair_width(k)] = part
        pair_copy(k, way).start()

    def wide(value):
        return value.astype(jnp.float32)

    def finish(chunk, total):
        _, start, width = chunk
        out_ref[:, start : start + width] = total.astype(jnp.bfloat16)

    def ring_step(k, way, step):
        ring_copy(k, way, step).wait_recv()
        at = block(way, step + 1)
        width = ring_width(k)
        total = wide(xp[way, k, at, :, :, :width]) + wide(xr[way, k, step, :, :, :width])
        xp[way, k, at, :, :, :width] = total.astype(jnp.bfloat16)
        if step < RING - 2:
            ring_copy(k, way, step + 1).start()
        else:
            ring_pair_copy(k, way).start()

    def ring_end(k, way):
        ring_pair_copy(k, way).wait_recv()
        width = ring_width(k)
        finish(
            chunks[(True, k, way)],
            wide(xp[way, k, x, z, :, :width]) + wide(xq[way, k, :, :width]),
        )

    def pair_step(k, way):
        pair_copy(k, way).wait_recv()
        at = block(way, 0)
        width = pair_width(k)
        total = wide(zp[way, k, z, at, :, :width]) + wide(zq[way, k, at, :, :width])
        zp[way, k, z, at, :, :width] = total.astype(jnp.bfloat16)
        pair_ring_copy(k, way, 0).start()

    def pair_ring_step(k, way, step):
        pair_ring_copy(k, way, step).wait_recv()
        at = block(way, step + 1)
        width = pair_width(k)
        total = wide(zp[way, k, z, at, :, :width]) + wide(zq[way, k, at, :, :width])
        total = total + wide(zr[way, k, step, :, :width])
        if step < RING - 2:
            zp[way, k, z, at, :, :width] = total.astype(jnp.bfloat16)
            pair_ring_copy(k, way, step + 1).start()
        else:
            finish(chunks[(False, k, way)], total)

    def begin():
        for kind, k, _ in ORDER:
            if kind in (START_RING, START_PAIR):
                for way in range(2):
                    fetch(chunks[(kind == START_RING, k, way)]).start()
        barrier = pltpu.get_barrier_semaphore()
        for device in (ring_device(0), ring_device(1), pair_device):
            pl.semaphore_signal(
                barrier, inc=1, device_id=device, device_id_type=pl.DeviceIdType.MESH
            )

    def run():
        for kind, k, step in ORDER:
            for way in range(2):
                if kind == START_RING:
                    start_ring(k, way)
                elif kind == START_PAIR:
                    start_pair(k, way)
                elif kind == RING_STEP:
                    ring_step(k, way, step)
                elif kind == RING_END:
                    ring_end(k, way)
                elif kind == PAIR_STEP:
                    pair_step(k, way)
                else:
                    pair_ring_step(k, way, step)
        for way in range(2):
            for k in range(RING_FIRST):
                for step in range(RING - 1):
                    ring_copy(k, way, step).wait_send()
                ring_pair_copy(k, way).wait_send()
            for k in range(PAIR_FIRST):
                pair_copy(k, way).wait_send()
                for step in range(RING - 1):
                    pair_ring_copy(k, way, step).wait_send()

    return begin, run


def kernel(heads, *refs):
    inputs, out_ref, scratch = refs[:5], refs[5], refs[6:]
    slot_prompt_ref, query_hbm, own_hbm, cache_hbm, weight_hbm = inputs
    attended_ref, exchange_scratch, project_scratch = scratch[0], scratch[1:15], scratch[15:]
    begin, run = project(attended_ref, weight_hbm, out_ref, *project_scratch)
    exchange(
        heads,
        begin,
        slot_prompt_ref,
        query_hbm,
        own_hbm,
        cache_hbm,
        attended_ref,
        *exchange_scratch,
    )
    run()


def attend_and_project(slot_prompt, query, own_rows, cache, out_weight, heads):
    prompts, query_rows, head_size = query.shape
    message = query_rows + 2 * OWN
    held = jnp.bfloat16
    dma = pltpu.SemaphoreType.DMA
    hbm = pl.BlockSpec(memory_space=pl.ANY)
    depth, columns = out_weight.shape
    total = own_rows.shape[0]
    rows = total // (2 * RING)
    chunks = 2 * (RING_FIRST + PAIR_FIRST)
    units = 2 * (sum(RING_UNITS) + sum(PAIR_UNITS))
    width = max(RING_UNITS + PAIR_UNITS) * columns // units
    steps = RING - 1
    return pl.pallas_call(
        functools.partial(kernel, heads),
        in_specs=[pl.BlockSpec(memory_space=pltpu.SMEM), hbm, hbm, hbm, hbm],
        out_specs=pl.BlockSpec(memory_space=pltpu.VMEM),
        out_shape=jax.ShapeDtypeStruct((rows, columns), held),
        scratch_shapes=[
            pltpu.VMEM((total, depth), held),
            pltpu.VMEM(query.shape, held),
            pltpu.VMEM((prompts, OWN, 2 * head_size), held),
            pltpu.VMEM(own_rows.shape, held),
            pltpu.VMEM(cache.shape, held),
            pltpu.VMEM((prompts, message, head_size), held),
            pltpu.VMEM((prompts, message, head_size), held),
            pltpu.VMEM(query.shape, held),
            pltpu.VMEM(query.shape, held),
            pltpu.SMEM((prompts,), jnp.int32),
            dma((3,)),
            dma,
            dma((Z_HI,)),
            dma,
            dma,
            pltpu.VMEM((chunks, depth, width), held),
            dma((chunks,)),
            pltpu.VMEM((2, RING_FIRST, RING, 2, rows, width), held),
            pltpu.VMEM((2, RING_FIRST, steps, 2, rows, width), held),
            pltpu.VMEM((2, RING_FIRST, rows, width), held),
            pltpu.VMEM((2, PAIR_FIRST, 2, RING, rows, width), held),
            pltpu.VMEM((2, PAIR_FIRST, RING, rows, width), held),
            pltpu.VMEM((2, PAIR_FIRST, steps, rows, width), held),
            dma((2, RING_FIRST, steps)),
            dma((2, RING_FIRST, steps)),
            dma((2, RING_FIRST)),
            dma((2, RING_FIRST)),
            dma((2, PAIR_FIRST)),
            dma((2, PAIR_FIRST)),
            dma((2, PAIR_FIRST, steps)),
            dma((2, PAIR_FIRST, steps)),
        ],
        compiler_params=pltpu.CompilerParams(
            collective_id=0, has_side_effects=True, vmem_limit_bytes=60 * 2**20
        ),
    )(slot_prompt, query, own_rows, cache, out_weight)


def on_device(queries, cache, new_kv, slot_prompt, residual, out_weight, gain):
    row_total, heads_local, head_size = queries.shape
    prompts = slot_prompt.shape[0]
    rows = row_total // prompts
    projected = attend_and_project(
        slot_prompt,
        queries.reshape(prompts, rows * heads_local, head_size),
        new_kv.reshape(row_total, 2 * head_size),
        cache.reshape(cache.shape[1], 2 * head_size),
        out_weight,
        heads_local,
    ).astype(jnp.float32)
    hidden = (residual.astype(jnp.float32) + projected).astype(jnp.bfloat16)
    hidden_f = hidden.astype(jnp.float32)
    spread = jnp.sqrt(jnp.mean(hidden_f * hidden_f, -1) + 1e-05)
    normed = (hidden_f / spread[:, None] * gain[None, :]).astype(jnp.bfloat16)
    return (hidden, normed)


def solution(mesh):
    placed = (
        P("samp", "tp", None),
        P("samp", None, "tp", None),
        P("samp", "tp", None),
        P(),
        P(("samp", "tp"), None),
        P("tp", None),
        P(),
    )
    return jax.shard_map(
        on_device,
        mesh=mesh,
        in_specs=placed,
        out_specs=(P(("samp", "tp"), None), P(("samp", "tp"), None)),
        check_vma=False,
    )
```
